512 devices in a mesh: grp: 16 (over y, z_lo), row: 32 (over z_hi, x, core).
Axes of the slice: x: 4, y: 8, z: 8 (z_hi: 4, z_lo: 2; z = z_hi * 2 + z_lo), core: 2. Of those that a mesh axis runs over, the one named last changes fastest.
Arguments:
- cov_prior: float32 [16384, 16384], P(('grp', 'row')), may hold values from -7 to 23, as said below
- courant_x_field: float32 [128, 128], replicated, may hold values from -0.35 to 0.35
- courant_y_field: float32 [128, 128], replicated, may hold values from -0.35 to 0.35
- obs_cells: int32 [2, 128], replicated, may hold values from 0 to 16383
- obs_var: float32 [2, 128], replicated, may hold values from 0.5 to 2
Outputs:
- analysis: float32 [16384, 16384], P('grp', 'row')
The draws below stay inside these ranges and needn't reach their ends.
Inputs may be any that keep to these rules, and one draw needn't show every extreme that they name: `cov_prior`: symmetric and positive definite. `obs_cells`: a cell may be observed more than once in an update.
All inputs are finite; a program needn't handle non-finite values.
Results may differ from the reference program's by a relative error of at most 0.0002.
Values sent between devices are 32-bit elements; how exact they have to be, the bound alone decides.
A program may use at most 64 MiB of HBM per device.

```python
import math
import jax
import jax.numpy as jnp
from jax import lax

ZONAL_POINTS = 128
NY = 128
NCELL = 16384
OBS = 128
UPDATES = 2
STEPS = 1


def draw_cov_prior(key, part):
    noise_key = jax.random.fold_in(key, 101)
    scale_key = jax.random.fold_in(key, 102)
    factor_key = jax.random.fold_in(key, 103)
    factor_count = 256
    cell_ids = jnp.arange(NCELL, dtype=jnp.int32)
    column_x = cell_ids % ZONAL_POINTS
    row_y = cell_ids // ZONAL_POINTS
    offsets = [(0, 1), (0, 2), (0, 3)] + [(shift_y, shift_x) for shift_y in (1, 2, 3) for shift_x in range(-3, 4)]
    band_noise = jax.random.uniform(noise_key, (len(offsets), NCELL), jnp.float32, -0.02, 0.02)
    scales = jnp.exp(jax.random.uniform(scale_key, (NCELL,), jnp.float32, 0.0, math.log(2.0)))
    loadings = jax.random.uniform(factor_key, (NCELL, factor_count), jnp.float32, -math.sqrt(3.0), math.sqrt(3.0))
    matrix = jnp.eye(NCELL, dtype=jnp.float32)
    for position, (shift_y, shift_x) in enumerate(offsets):
        inside = (column_x + shift_x >= 0) & (column_x + shift_x < ZONAL_POINTS) & (row_y + shift_y < NY)
        target = jnp.where(inside, cell_ids + shift_y * ZONAL_POINTS + shift_x, cell_ids)
        amount = jnp.where(inside, band_noise[position], 0.0)
        matrix = matrix.at[cell_ids, target].add(amount)
        matrix = matrix.at[target, cell_ids].add(amount)
    shared = jnp.dot(loadings, loadings.T, precision=lax.Precision.HIGHEST) * (0.5 / factor_count)
    matrix = matrix + shared
    return matrix * scales[:, None] * scales[None, :]


def place_ends(values, rng, least, largest):
    dims = values.shape
    place = [jax.random.randint(jax.random.fold_in(rng, axis), (), 0, dims[axis]) for axis in range(len(dims))]
    values = values.at[tuple(place)].set(least)
    longest = dims.index(max(dims))
    place[longest] = (place[longest] + 1) % dims[longest]
    return values.at[tuple(place)].set(largest)


def setup_inputs(seed: int = 0) -> dict:
    key_of = jax.random.split(jax.random.key(seed), 6)
    cov_prior = draw_cov_prior(jax.random.fold_in(key_of[5], 71), 0)
    courant_x_field = jnp.clip(jax.random.uniform(key_of[1], (NY, ZONAL_POINTS), jnp.float32, -0.35, 0.35), -0.35, 0.35)
    courant_y_field = jnp.clip(jax.random.uniform(key_of[2], (NY, ZONAL_POINTS), jnp.float32, -0.35, 0.35), -0.35, 0.35)
    obs_cells = place_ends(jax.random.randint(key_of[3], (UPDATES, OBS), 0, NCELL), jax.random.fold_in(key_of[3], 1), 0, NCELL - 1).astype(jnp.int32)
    obs_var = jnp.clip(jnp.exp(jax.random.uniform(key_of[4], (UPDATES, OBS), jnp.float32, math.log(0.5), math.log(2.0))), 0.5, 2.0)
    return {"cov_prior": cov_prior, "courant_x_field": courant_x_field, "courant_y_field": courant_y_field, "obs_cells": obs_cells, "obs_var": obs_var}


diffusion = 0.1

def tendency(padded, u_part, v_part):
    middle = padded[:, 2:-2]
    center = middle[:, :, 2:-2]
    along_x = (8.0 * (middle[:, :, 3:-1] - middle[:, :, 1:-3]) - (middle[:, :, 4:] - middle[:, :, :-4])) / 12.0
    column = padded[:, :, 2:-2]
    along_y = (8.0 * (column[:, 3:-1] - column[:, 1:-3]) - (column[:, 4:] - column[:, :-4])) / 12.0
    laplace = middle[:, :, 3:-1] + middle[:, :, 1:-3] + column[:, 3:-1] + column[:, 1:-3] - 4.0 * center
    return diffusion * laplace - u_part * along_x - v_part * along_y

def heun_step(fields, courant_x_field, courant_y_field):
    slope_first = tendency(jnp.pad(fields, ((0, 0), (2, 2), (2, 2))), courant_x_field, courant_y_field)
    latter_increment = tendency(jnp.pad(fields + slope_first, ((0, 0), (2, 2), (2, 2))), courant_x_field, courant_y_field)
    return fields + 0.5 * (slope_first + latter_increment)

def propagate(matrix, courant_x_field, courant_y_field):
    row_count = matrix.shape[0]
    meridional_count = min(512, row_count)

    def advance_block(stacked):
        for repeat in range(STEPS):
            stacked = heun_step(stacked, courant_x_field, courant_y_field)
        return stacked
    blocks = matrix.reshape(row_count // meridional_count, meridional_count, NY, ZONAL_POINTS)
    return lax.map(advance_block, blocks).reshape(row_count, NCELL)

def reference(cov_prior, courant_x_field, courant_y_field, obs_cells, obs_var):
    advanced = propagate(cov_prior, courant_x_field, courant_y_field)
    posterior_mean = propagate(advanced.T, courant_x_field, courant_y_field).T
    for update_number in range(UPDATES):
        picked = obs_cells[update_number]
        observed_rows = posterior_mean[picked, :]
        observed_cols = posterior_mean[:, picked]
        inner_block = observed_rows[:, picked]
        system = 0.5 * (inner_block + inner_block.T) + jnp.diag(obs_var[update_number])
        factor = jnp.linalg.cholesky(system)
        halfway = lax.linalg.triangular_solve(factor, observed_rows, left_side=True, lower=True)
        weights = lax.linalg.triangular_solve(factor, halfway, left_side=True, lower=True, transpose_a=True)
        posterior_mean = posterior_mean - jnp.dot(observed_cols, weights, precision=lax.Precision.HIGHEST)
    return posterior_mean
```

```python
import functools

import jax
import jax.numpy as jnp
from jax import lax
from jax.experimental import pallas as pl
from jax.experimental.pallas import tpu as pltpu
from jax.sharding import PartitionSpec as P

NX = 128
NY = 128
NCELL = NX * NY
OBS = 256
GROUPS = 16
MEMBERS = 32
ROWS = 32
HIGHEST = lax.Precision.HIGHEST
MESH = pl.DeviceIdType.MESH
VMEM = pl.BlockSpec(memory_space=pltpu.VMEM)
SMEM = pl.BlockSpec(memory_space=pltpu.SMEM)
VMEM_LIMIT = 48 * 1024 * 1024


def stencil_coefficients(u, v):
    x = lax.broadcasted_iota(jnp.int32, (NY, NX), 1)
    y = lax.broadcasted_iota(jnp.int32, (NY, NX), 0)
    u12 = u / 12.0
    v12 = v / 12.0
    return jnp.stack(
        [
            jnp.where(x < NX - 1, 0.1 - 8.0 * u12, 0.0),
            jnp.where(x > 0, 0.1 + 8.0 * u12, 0.0),
            jnp.where(x < NX - 2, u12, 0.0),
            jnp.where(x > 1, -u12, 0.0),
            jnp.where(y < NY - 1, 0.1 - 8.0 * v12, 0.0),
            jnp.where(y > 0, 0.1 + 8.0 * v12, 0.0),
            jnp.where(y < NY - 2, v12, 0.0),
            jnp.where(y > 1, -v12, 0.0),
        ],
        axis=1,
    )


def lane_slope(cf, q, yp1, ym1, yp2, ym2):
    return (
        cf[0:1] * pltpu.roll(q, NX - 1, 1)
        + cf[1:2] * pltpu.roll(q, 1, 1)
        + cf[2:3] * pltpu.roll(q, NX - 2, 1)
        + cf[3:4] * pltpu.roll(q, 2, 1)
        + cf[4:5] * yp1
        + cf[5:6] * ym1
        + cf[6:7] * yp2
        + cf[7:8] * ym2
        - 0.4 * q
    )


def lanes(y):
    return pl.ds(pl.multiple_of(y * NX, NX), NX)


def rows_kernel(obs_ref, c_ref, coef_ref, a_ref, aot_ref, q1_ref):
    def read(ref, y):
        return ref[:, lanes(jnp.clip(y, 0, NY - 1))]

    def slope(ref, y):
        return lane_slope(
            coef_ref[y],
            read(ref, y),
            read(ref, y + 1),
            read(ref, y - 1),
            read(ref, y + 2),
            read(ref, y - 2),
        )

    def first(y, carry):
        q1_ref[:, lanes(y)] = c_ref[:, lanes(y)] + slope(c_ref, y)
        return carry

    def second(y, carry):
        a_ref[:, lanes(y)] = 0.5 * (c_ref[:, lanes(y)] + q1_ref[:, lanes(y)] + slope(q1_ref, y))
        return carry

    lax.fori_loop(0, NY, first, 0, unroll=4)
    lax.fori_loop(0, NY, second, 0, unroll=4)

    lane = lax.broadcasted_iota(jnp.int32, (ROWS, NX), 1)
    quarter = lax.axis_index("row") % 4
    place = lax.broadcasted_iota(jnp.int32, (NX, NX), 0) // ROWS == quarter
    for update in range(2):

        def pick(j, acc):
            cell = obs_ref[update, j]
            block = a_ref[:, lanes(cell // NX)]
            turned = pltpu.roll(block, (j - cell % NX + NX) % NX, 1)
            return jnp.where(lane == j, turned, acc)

        acc = lax.fori_loop(0, NX, pick, jnp.zeros((ROWS, NX), jnp.float32), unroll=8)
        full = jnp.where(place, jnp.concatenate([acc] * 4, axis=0), 0.0)
        aot_ref[update * NX : (update + 1) * NX, :] = full.T


def advance_rows(obs_cells, cov, coefs):
    return pl.pallas_call(
        rows_kernel,
        out_shape=(
            jax.ShapeDtypeStruct((ROWS, NCELL), jnp.float32),
            jax.ShapeDtypeStruct((OBS, NX), jnp.float32),
        ),
        in_specs=[SMEM, VMEM, VMEM],
        out_specs=(VMEM, VMEM),
        scratch_shapes=[pltpu.VMEM((ROWS, NCELL), jnp.float32)],
        compiler_params=pltpu.CompilerParams(vmem_limit_bytes=VMEM_LIMIT),
    )(obs_cells, cov, coefs)


def drain(ref, sem):
    pltpu.make_async_copy(ref, ref, sem).wait()


def remote(src, dst, send_sem, recv_sem, grp, row):
    return pltpu.make_async_remote_copy(
        src_ref=src,
        dst_ref=dst,
        send_sem=send_sem,
        recv_sem=recv_sem,
        device_id={"grp": grp, "row": row},
        device_id_type=MESH,
    )


def chain_kernel(
    obs_ref, aot_ref, coef_ref, s_ref, yg_ref, yr_ref,
    pieces, ext, mid, yt, spart, sparts, srow, send_sem, recv_sem,
):
    g = lax.axis_index("grp")
    r = lax.axis_index("row")
    y_in, quarter = r // 4, r % 4
    low = y_in < 4

    def share(i, carry):
        to = lax.rem(r + i, MEMBERS)
        remote(
            aot_ref.at[pl.ds(pl.multiple_of(to * 8, 8), 8)],
            pieces.at[16 + r], send_sem.at[0], recv_sem.at[0], g, to,
        ).start()
        return carry

    lax.fori_loop(1, MEMBERS, share, 0)
    own = pltpu.make_async_copy(
        aot_ref.at[pl.ds(pl.multiple_of(r * 8, 8), 8)], pieces.at[16 + r], recv_sem.at[0]
    )
    own.start()
    side = jnp.where(low, g - 1, g + 1)
    slot = jnp.where(low, 12 + y_in, y_in - 4) * 4 + quarter
    has_side = (side >= 0) & (side < GROUPS)

    @pl.when(has_side)
    def _():
        def share_side(i, carry):
            to = lax.rem(r + i, MEMBERS)
            remote(
                aot_ref.at[pl.ds(pl.multiple_of(to * 8, 8), 8)],
                pieces.at[slot], send_sem.at[1], recv_sem.at[jnp.where(low, 2, 1)], side, to,
            ).start()
            return carry

        lax.fori_loop(0, MEMBERS, share_side, 0)

    @pl.when(g == 0)
    def _():
        pieces[0:16] = jnp.zeros((16, 8, NX), jnp.float32)

    @pl.when(g == GROUPS - 1)
    def _():
        pieces[48:64] = jnp.zeros((16, 8, NX), jnp.float32)

    drain(pieces.at[16:48], recv_sem.at[0])

    @pl.when(g > 0)
    def _():
        drain(pieces.at[0:16], recv_sem.at[1])

    @pl.when(g < GROUPS - 1)
    def _():
        drain(pieces.at[48:64], recv_sem.at[2])

    for y in range(16):
        ext[:, y * NX : (y + 1) * NX] = (
            pieces[4 * y] + pieces[4 * y + 1] + pieces[4 * y + 2] + pieces[4 * y + 3]
        )

    def at(ref, y):
        return ref[:, y * NX : (y + 1) * NX]

    def slope(ref, y):
        return lane_slope(
            coef_ref[y], at(ref, y), at(ref, y + 1), at(ref, y - 1), at(ref, y + 2), at(ref, y - 2)
        )

    for y in range(2, 14):
        mid[:, y * NX : (y + 1) * NX] = at(ext, y) + slope(ext, y)
    for y in range(4, 12):
        yt[:, (y - 4) * NX : (y - 3) * NX] = 0.5 * (at(ext, y) + at(mid, y) + slope(mid, y))

    yg_ref[r] = yt[...]

    def to_group(i, carry):
        to = lax.rem(r + i, MEMBERS)
        remote(yt, yg_ref.at[r], send_sem.at[2], recv_sem.at[3], g, to).start()
        return carry

    def to_columns(i, carry):
        grp = lax.rem(g + i // 2, GROUPS)
        row = 2 * g + i % 2
        src = yt.at[:, pl.ds(pl.multiple_of((i % 2) * 512, 512), 512)]
        here = (grp == g) & (row == r)

        @pl.when(here)
        def _():
            pltpu.make_async_copy(src, yr_ref.at[r], recv_sem.at[4]).start()

        @pl.when(jnp.logical_not(here))
        def _():
            remote(src, yr_ref.at[r], send_sem.at[3], recv_sem.at[4], grp, row).start()

        return carry

    cell = lax.broadcasted_iota(jnp.int32, (1024, OBS), 0)
    chosen = jnp.where(cell == obs_ref[...] - 1024 * g, 1.0, 0.0)
    spart[...] = jnp.dot(yt[...], chosen, precision=HIGHEST, preferred_element_type=jnp.float32)
    sparts[g] = spart[...]

    def to_groups(i, carry):
        to = lax.rem(g + i, GROUPS)
        remote(spart, sparts.at[g], send_sem.at[4], recv_sem.at[5], to, r).start()
        return carry

    lax.fori_loop(1, GROUPS, to_groups, 0)
    lax.fori_loop(1, MEMBERS, to_group, 0)
    lax.fori_loop(0, MEMBERS, to_columns, 0)
    drain(sparts.at[0:15], recv_sem.at[5])
    srow[...] = jnp.sum(sparts[...], axis=0)
    s_ref[r] = srow[...]

    def block_row(i, carry):
        to = lax.rem(r + i, MEMBERS)
        remote(srow, s_ref.at[r], send_sem.at[5], recv_sem.at[6], g, to).start()
        return carry

    lax.fori_loop(1, MEMBERS, block_row, 0)
    drain(s_ref.at[0:31], recv_sem.at[6])
    drain(yg_ref.at[0:31], recv_sem.at[3])
    drain(yr_ref.at[0:32], recv_sem.at[4])

    drain(pieces.at[0:31], send_sem.at[0])

    @pl.when(has_side)
    def _():
        drain(pieces.at[0:32], send_sem.at[1])

    drain(yg_ref.at[0:31], send_sem.at[2])

    @pl.when(r // 2 == g)
    def _():
        drain(yr_ref.at[0:31], send_sem.at[3])

    @pl.when(r // 2 != g)
    def _():
        drain(yr_ref.at[0:32], send_sem.at[3])

    drain(sparts.at[0:15], send_sem.at[4])
    drain(s_ref.at[0:31], send_sem.at[5])


def observation_chain(obs_row, aot, coef_ext):
    return pl.pallas_call(
        chain_kernel,
        out_shape=(
            jax.ShapeDtypeStruct((MEMBERS, 8, OBS), jnp.float32),
            jax.ShapeDtypeStruct((MEMBERS, 8, 1024), jnp.float32),
            jax.ShapeDtypeStruct((MEMBERS, 8, 512), jnp.float32),
        ),
        in_specs=[VMEM] * 3,
        out_specs=(VMEM,) * 3,
        scratch_shapes=[
            pltpu.VMEM((64, 8, NX), jnp.float32),
            pltpu.VMEM((8, 2048), jnp.float32),
            pltpu.VMEM((8, 2048), jnp.float32),
            pltpu.VMEM((8, 1024), jnp.float32),
            pltpu.VMEM((8, OBS), jnp.float32),
            pltpu.VMEM((GROUPS, 8, OBS), jnp.float32),
            pltpu.VMEM((8, OBS), jnp.float32),
            pltpu.SemaphoreType.DMA((6,)),
            pltpu.SemaphoreType.DMA((7,)),
        ],
        compiler_params=pltpu.CompilerParams(
            has_side_effects=True, vmem_limit_bytes=VMEM_LIMIT
        ),
    )(obs_row, aot, coef_ext)


def negative_inverse(ref):
    row_at = lax.broadcasted_iota(jnp.int32, (128, 128), 0)
    col_at = lax.broadcasted_iota(jnp.int32, (128, 128), 1)

    def step(k, carry):
        a = ref[...]
        row = ref[pl.ds(k, 1), :]
        in_col = col_at == k
        col = jnp.sum(jnp.where(in_col, a, 0.0), axis=1, keepdims=True)
        pivot = jnp.sum(jnp.where(in_col[0:1], row, 0.0), axis=1, keepdims=True)
        inv = 1.0 / pivot
        scaled = row * inv
        new = a - col * scaled
        new = jnp.where(in_col, col * inv, new)
        ref[...] = jnp.where(row_at == k, jnp.where(in_col[0:1], -inv, scaled), new)
        return carry

    lax.fori_loop(0, 128, step, 0)


def dot(a, b):
    return jnp.dot(a, b, precision=HIGHEST, preferred_element_type=jnp.float32)


def solve_kernel(s_ref, r_ref, var_ref, z_ref, first, second):
    diagonal = lax.broadcasted_iota(jnp.int32, (128, 128), 0) == lax.broadcasted_iota(
        jnp.int32, (128, 128), 1
    )
    s11 = s_ref[0:128, 0:128]
    s12 = s_ref[0:128, 128:256]
    s21 = s_ref[128:256, 0:128]
    s22 = s_ref[128:256, 128:256]
    first[...] = 0.5 * (s11 + s11.T) + jnp.where(diagonal, var_ref[0:1, :], 0.0)
    negative_inverse(first)
    inner = s22 + dot(s21, dot(first[...], s12))
    second[...] = 0.5 * (inner + inner.T) + jnp.where(diagonal, var_ref[1:2, :], 0.0)
    negative_inverse(second)
    r1 = r_ref[0:128, :]
    r2 = r_ref[128:256, :] + dot(s21, dot(first[...], r1))
    z2 = -dot(second[...], r2)
    z_ref[128:256, :] = z2
    z_ref[0:128, :] = -dot(first[...], r1 - dot(s12, z2))


def solve(s, r, var):
    return pl.pallas_call(
        solve_kernel,
        out_shape=jax.ShapeDtypeStruct((OBS, 512), jnp.float32),
        in_specs=[VMEM] * 3,
        out_specs=VMEM,
        scratch_shapes=[pltpu.VMEM((128, 128), jnp.float32)] * 2,
        compiler_params=pltpu.CompilerParams(vmem_limit_bytes=VMEM_LIMIT),
    )(s, r, var)


def column_slope(q, yp1, ym1, yp2, ym2, u12, v12):
    x = lax.broadcasted_iota(jnp.int32, (NX, NX), 0)
    xp1 = jnp.where(x < NX - 1, pltpu.roll(q, NX - 1, 0), 0.0)
    xm1 = jnp.where(x > 0, pltpu.roll(q, 1, 0), 0.0)
    xp2 = jnp.where(x < NX - 2, pltpu.roll(q, NX - 2, 0), 0.0)
    xm2 = jnp.where(x > 1, pltpu.roll(q, 2, 0), 0.0)
    along_x = 8.0 * (xp1 - xm1) - (xp2 - xm2)
    along_y = 8.0 * (yp1 - ym1) - (yp2 - ym2)
    laplace = xp1 + xm1 + yp1 + ym1 - 4.0 * q
    return 0.1 * laplace - u12 * along_x - v12 * along_y


def main_kernel(
    a_ref, u_ref, v_ref, yg_ref, z_ref, out_ref,
    ext, mid, fore, theirs, ub, vb, qh, ql, zh, zl_, send_sem, recv_sem,
):
    g = lax.axis_index("grp")
    r = lax.axis_index("row")
    y, lo = g // 2, g % 2
    me = lo * MEMBERS + r

    for c in range(2):

        def scatter(i, carry):
            to = lax.rem(me + i, 2 * MEMBERS)
            to_lo, to_r = to // MEMBERS, to % MEMBERS
            start = pl.multiple_of(to_r * 512 + to_lo * 256 + c * 128, 128)
            remote(
                a_ref.at[:, pl.ds(start, 128)], ext.at[c, 16 + me],
                send_sem.at[c], recv_sem.at[c], 2 * y + to_lo, to_r,
            ).start()
            return carry

        lax.fori_loop(1, 2 * MEMBERS, scatter, 0)
        pltpu.make_async_copy(
            a_ref.at[:, pl.ds(pl.multiple_of(r * 512 + lo * 256 + c * 128, 128), 128)],
            ext.at[c, 16 + me], recv_sem.at[c],
        ).start()

    for yy in range(20):
        ub[yy] = jnp.broadcast_to(u_ref[:, yy : yy + 1], (NX, NX))
        vb[yy] = jnp.broadcast_to(v_ref[:, yy : yy + 1], (NX, NX))
    for j in range(8):
        q = yg_ref[:, j * NX : (j + 1) * NX].T
        high = q.astype(jnp.bfloat16)
        qh[j] = high
        ql[j] = (q - high.astype(jnp.float32)).astype(jnp.bfloat16)
    z = z_ref[...]
    z_high = z.astype(jnp.bfloat16)
    zh[...] = z_high
    zl_[...] = (z - z_high.astype(jnp.float32)).astype(jnp.bfloat16)

    @pl.when(y == 0)
    def _():
        for c in range(2):
            ext[c, 0:16] = jnp.zeros((16, ROWS, NX), jnp.float32)

    @pl.when(y == 7)
    def _():
        for c in range(2):
            ext[c, 80:96] = jnp.zeros((16, ROWS, NX), jnp.float32)

    def up(c):
        return remote(
            ext.at[c, 64:80], ext.at[c, 0:16], send_sem.at[2 + c], recv_sem.at[2 + c], g + 2, r
        )

    def down(c):
        return remote(
            ext.at[c, 16:32], ext.at[c, 80:96], send_sem.at[4 + c], recv_sem.at[4 + c], g - 2, r
        )

    def trade(c):
        return remote(
            fore.at[c, 1 - lo], theirs.at[c], send_sem.at[6 + c], recv_sem.at[6 + c],
            2 * y + 1 - lo, r,
        )

    def grid_row(c, yy):
        return jnp.concatenate([ext[c, 4 * yy + k] for k in range(4)], axis=0)

    def correct(column, j, field):
        at = pl.ds(column, 128)
        a_high, a_low, b_high, b_low = qh[j], ql[j], zh[:, at], zl_[:, at]

        def part(a, b):
            return jnp.dot(a, b, preferred_element_type=jnp.float32)

        out_ref[pl.ds(pl.multiple_of(j * NX, NX), NX), at] = field - (
            part(a_high, b_high) + part(a_high, b_low) + part(a_low, b_high)
        )

    for c in range(2):
        drain(ext.at[c, 16:80], recv_sem.at[c])

        @pl.when(y < 7)
        def _():
            up(c).start()

        @pl.when(y > 0)
        def _():
            down(c).start()

    for c in range(2):

        @pl.when(y > 0)
        def _():
            up(c).wait_recv()

        @pl.when(y < 7)
        def _():
            down(c).wait_recv()

        def first(yy, carry):
            q = grid_row(c, yy)
            inside = (y * 16 + yy - 4 >= 0) & (y * 16 + yy - 4 < NY)
            step = column_slope(
                q, grid_row(c, yy + 1), grid_row(c, yy - 1), grid_row(c, yy + 2),
                grid_row(c, yy - 2), ub[yy - 2], vb[yy - 2],
            )
            mid[yy - 2] = jnp.where(inside, q + step, 0.0)
            return carry

        def second(yy, carry):
            q1 = mid[yy - 2]
            step = column_slope(
                q1, mid[yy - 1], mid[yy - 3], mid[yy], mid[yy - 4], ub[yy - 2], vb[yy - 2]
            )
            at = yy - 4
            fore[c, at // 8, at % 8] = 0.5 * (grid_row(c, yy) + q1 + step)
            return carry

        lax.fori_loop(2, 22, first, 0)
        lax.fori_loop(4, 20, second, 0)
        trade(c).start()
        mine = pl.multiple_of(lo * 256 + c * 128, 128)

        def finish(j, carry):
            correct(mine, j, fore[c, lo, j])
            return carry

        lax.fori_loop(0, 8, finish, 0)

    for c in range(2):
        trade(c).wait_recv()
        other = pl.multiple_of((1 - lo) * 256 + c * 128, 128)

        def finish_other(j, carry):
            correct(other, j, theirs[c, j])
            return carry

        lax.fori_loop(0, 8, finish_other, 0)

    for c in range(2):
        drain(ext.at[c, 0:63], send_sem.at[c])
        trade(c).wait_send()

        @pl.when(y < 7)
        def _():
            up(c).wait_send()

        @pl.when(y > 0)
        def _():
            down(c).wait_send()


def exchange_and_correct(a, u_ext, v_ext, yg, z):
    f32, bf16 = jnp.float32, jnp.bfloat16
    return pl.pallas_call(
        main_kernel,
        out_shape=jax.ShapeDtypeStruct((1024, 512), f32),
        in_specs=[VMEM] * 5,
        out_specs=VMEM,
        scratch_shapes=[
            pltpu.VMEM((2, 96, ROWS, NX), f32),
            pltpu.VMEM((20, NX, NX), f32),
            pltpu.VMEM((2, 2, 8, NX, NX), f32),
            pltpu.VMEM((2, 8, NX, NX), f32),
            pltpu.VMEM((20, NX, NX), f32),
            pltpu.VMEM((20, NX, NX), f32),
            pltpu.VMEM((8, NX, OBS), bf16),
            pltpu.VMEM((8, NX, OBS), bf16),
            pltpu.VMEM((OBS, 512), bf16),
            pltpu.VMEM((OBS, 512), bf16),
            pltpu.SemaphoreType.DMA((8,)),
            pltpu.SemaphoreType.DMA((8,)),
        ],
        compiler_params=pltpu.CompilerParams(
            has_side_effects=True, vmem_limit_bytes=VMEM_LIMIT
        ),
    )(a, u_ext, v_ext, yg, z)


def local(cov_prior, courant_x_field, courant_y_field, obs_cells, obs_var):
    g = lax.axis_index("grp")
    coefs = stencil_coefficients(courant_x_field, courant_y_field)
    advanced, aot = advance_rows(obs_cells, cov_prior, coefs)
    coef_ext = lax.dynamic_slice_in_dim(
        jnp.pad(coefs, ((4, 4), (0, 0), (0, 0))), g * 8, 16, 0
    )
    s, yg, yr = observation_chain(obs_cells.reshape(1, OBS), aot, coef_ext)
    z = solve(s.reshape(OBS, OBS), yr.reshape(OBS, 512), obs_var)

    def columns(field):
        padded = jnp.pad(field / 12.0, ((2, 2), (0, 0)))
        return lax.dynamic_slice_in_dim(padded, (g // 2) * 16, 20, 0).T

    return exchange_and_correct(
        advanced, columns(courant_x_field), columns(courant_y_field), yg.reshape(OBS, 1024), z
    )


def solution(mesh):
    placed = (P(("grp", "row"), None), P(), P(), P(), P())
    return jax.shard_map(
        local, mesh=mesh, in_specs=placed, out_specs=P("grp", "row"), check_vma=False
    )
```

```python
import jax
import jax.numpy as jnp
from jax import lax
from jax.experimental import pallas as pl
from jax.experimental.pallas import tpu as pltpu
from jax.sharding import PartitionSpec as P

NX = 128
NY = 128
NCELL = NX * NY
OBS = 256
GROUPS = 16
MEMBERS = 32
ROWS = 32
HIGHEST = lax.Precision.HIGHEST
MESH = pl.DeviceIdType.MESH
VMEM = pl.BlockSpec(memory_space=pltpu.VMEM)
VMEM_LIMIT = 48 * 1024 * 1024


def lane_slope(cf, q, yp1, ym1, yp2, ym2):
    return (
        cf[0] * pltpu.roll(q, NX - 1, 1)
        + cf[1] * pltpu.roll(q, 1, 1)
        + cf[2] * pltpu.roll(q, NX - 2, 1)
        + cf[3] * pltpu.roll(q, 2, 1)
        + cf[4] * yp1
        + cf[5] * ym1
        + cf[6] * yp2
        + cf[7] * ym2
        - 0.4 * q
    )


def lanes(y):
    return pl.ds(pl.multiple_of(y * NX, NX), NX)


def drain(ref, sem):
    pltpu.make_async_copy(ref, ref, sem).wait()


def remote(src, dst, send_sem, recv_sem, grp, row):
    return pltpu.make_async_remote_copy(
        src_ref=src,
        dst_ref=dst,
        send_sem=send_sem,
        recv_sem=recv_sem,
        device_id={"grp": grp, "row": row},
        device_id_type=MESH,
    )


def negative_inverse(ref):
    row_at = lax.broadcasted_iota(jnp.int32, (128, 128), 0)
    col_at = lax.broadcasted_iota(jnp.int32, (128, 128), 1)

    def step(k, carry):
        a = ref[...]
        row = ref[pl.ds(k, 1), :]
        in_col = col_at == k
        col = jnp.sum(jnp.where(in_col, a, 0.0), axis=1, keepdims=True)
        pivot = jnp.sum(jnp.where(in_col[0:1], row, 0.0), axis=1, keepdims=True)
        inv = 1.0 / pivot
        scaled = row * inv
        new = a - col * scaled
        new = jnp.where(in_col, col * inv, new)
        ref[...] = jnp.where(row_at == k, jnp.where(in_col[0:1], -inv, scaled), new)
        return carry

    lax.fori_loop(0, 128, step, 0)


def dot(a, b):
    return jnp.dot(a, b, precision=HIGHEST, preferred_element_type=jnp.float32)


def dot(a, b):
    return jnp.dot(a, b, precision=HIGHEST, preferred_element_type=jnp.float32)


def column_slope(q, yp1, ym1, yp2, ym2, u12, v12):
    x = lax.broadcasted_iota(jnp.int32, (NX, NX), 0)
    xp1 = jnp.where(x < NX - 1, pltpu.roll(q, NX - 1, 0), 0.0)
    xm1 = jnp.where(x > 0, pltpu.roll(q, 1, 0), 0.0)
    xp2 = jnp.where(x < NX - 2, pltpu.roll(q, NX - 2, 0), 0.0)
    xm2 = jnp.where(x > 1, pltpu.roll(q, 2, 0), 0.0)
    along_x = 8.0 * (xp1 - xm1) - (xp2 - xm2)
    along_y = 8.0 * (yp1 - ym1) - (yp2 - ym2)
    laplace = xp1 + xm1 + yp1 + ym1 - 4.0 * q
    return 0.1 * laplace - u12 * along_x - v12 * along_y


def kernel(
    obs_row_ref, c_ref, u_ref, v_ref, var_ref, out_ref,
    coef, q1, adv, aot, pieces, near, mid8, yt, rt, spart, sparts, srow, s_all, yg, yr, first, second,
    ext, mid, fore, theirs, ub, vb, qh, ql, zh, zl, send_sem, recv_sem,
):
    f32, bf16 = jnp.float32, jnp.bfloat16
    g = lax.axis_index("grp")
    r = lax.axis_index("row")
    y, lo = g // 2, g % 2
    chip, core = r // 2, r % 2
    me = lo * MEMBERS + r

    barrier = pltpu.get_barrier_semaphore()

    def greet(grp, row):
        pl.semaphore_signal(
            barrier, inc=1, device_id={"grp": grp, "row": row}, device_id_type=MESH
        )

    def greet_plane(i, carry):
        to = lax.rem(me + i, 2 * MEMBERS)
        greet(2 * y + to // MEMBERS, to % MEMBERS)
        return carry

    lax.fori_loop(1, 2 * MEMBERS, greet_plane, 0)
    across = jnp.where(lo == 0, g - 1, g + 1)
    has_across = (across >= 0) & (across < GROUPS)

    @pl.when(has_across)
    def _():
        def greet_across(i, carry):
            greet(across, i)
            return carry

        lax.fori_loop(0, MEMBERS, greet_across, 0)

    def greet_planes(i, carry):
        greet(lax.rem(2 * y + 2 + i // 2, GROUPS), 2 * chip + i % 2)
        return carry

    lax.fori_loop(0, 2 * GROUPS - 4, greet_planes, 0)
    on_diagonal = chip == g

    @pl.when(jnp.logical_not(on_diagonal))
    def _():
        greet(chip, 2 * g + core)

    gx = lax.broadcasted_iota(jnp.int32, (NY, NX), 1)
    gy = lax.broadcasted_iota(jnp.int32, (NY, NX), 0)
    u12 = u_ref[...] * (1.0 / 12.0)
    v12 = v_ref[...] * (1.0 / 12.0)
    factors = (
        jnp.where(gx < NX - 1, 0.1 - 8.0 * u12, 0.0),
        jnp.where(gx > 0, 0.1 + 8.0 * u12, 0.0),
        jnp.where(gx < NX - 2, u12, 0.0),
        jnp.where(gx > 1, -u12, 0.0),
        jnp.where(gy < NY - 1, 0.1 - 8.0 * v12, 0.0),
        jnp.where(gy > 0, 0.1 + 8.0 * v12, 0.0),
        jnp.where(gy < NY - 2, v12, 0.0),
        jnp.where(gy > 1, -v12, 0.0),
    )
    for k in range(8):
        coef[k, 0:8] = jnp.zeros((8, NX), f32)
        coef[k, 128:136] = jnp.zeros((8, NX), f32)
        coef[k, 4 : 4 + NY] = factors[k]

    def factors_at(row):
        return [coef[k, pl.ds(row, 1), :] for k in range(8)]

    def read(ref, yy):
        return ref[:, lanes(jnp.clip(yy, 0, NY - 1))]

    def row_slope(ref, yy):
        return lane_slope(
            factors_at(yy + 4), read(ref, yy), read(ref, yy + 1), read(ref, yy - 1),
            read(ref, yy + 2), read(ref, yy - 2),
        )

    def row_first(yy, carry):
        q1[:, lanes(yy)] = c_ref[:, lanes(yy)] + row_slope(c_ref, yy)
        return carry

    cells = obs_row_ref[...]
    chosen_x = jnp.where(
        lax.broadcasted_iota(jnp.int32, (NX, OBS), 0) == cells % NX, 1.0, 0.0
    ).astype(bf16)
    cells_y = cells // NX

    def row_second(yy, acc):
        new = 0.5 * (c_ref[:, lanes(yy)] + q1[:, lanes(yy)] + row_slope(q1, yy))
        adv[:, lanes(yy)] = new
        high = new.astype(bf16)
        rest = new - high.astype(f32)
        middle = rest.astype(bf16)
        low = (rest - middle.astype(f32)).astype(bf16)
        parts = jnp.dot(
            jnp.concatenate([high, middle, low], axis=0), chosen_x, preferred_element_type=f32
        )
        found = parts[0:ROWS] + (parts[ROWS : 2 * ROWS] + parts[2 * ROWS :])
        return jnp.where(cells_y == yy, found, acc)

    lax.fori_loop(0, NY, row_first, 0, unroll=4)
    acc = lax.fori_loop(0, NY, row_second, jnp.zeros((ROWS, OBS), f32), unroll=4)

    quarter = r % 4
    place = lax.broadcasted_iota(jnp.int32, (NX, NX), 0) // ROWS == quarter
    for update in range(2):
        part = acc[:, update * NX : (update + 1) * NX]
        full = jnp.where(place, jnp.concatenate([part] * 4, axis=0), 0.0)
        aot[update * NX : (update + 1) * NX, :] = full.T

    pl.semaphore_wait(
        barrier,
        2 * MEMBERS - 1 + 2 * GROUPS - 4
        + jnp.where(has_across, MEMBERS, 0) + jnp.where(on_diagonal, 0, 1),
    )

    def some(to):
        return aot.at[pl.ds(pl.multiple_of(to * 8, 8), 8)]

    def share(i, carry):
        to = lax.rem(r + i, MEMBERS)
        remote(some(to), pieces.at[16 + r], send_sem.at[0], recv_sem.at[0], g, to).start()
        return carry

    lax.fori_loop(1, MEMBERS, share, 0)
    pltpu.make_async_copy(some(r), pieces.at[16 + r], recv_sem.at[0]).start()
    y_in = r // 4
    low = y_in < 4
    side = jnp.where(low, g - 1, g + 1)
    slot = jnp.where(low, 12 + y_in, y_in - 4) * 4 + quarter
    has_side = (side >= 0) & (side < GROUPS)

    @pl.when(has_side)
    def _():
        def share_side(i, carry):
            to = lax.rem(r + i, MEMBERS)
            remote(
                some(to), pieces.at[slot], send_sem.at[1], recv_sem.at[jnp.where(low, 2, 1)], side, to
            ).start()
            return carry

        lax.fori_loop(0, MEMBERS, share_side, 0)

    def my_columns(c):
        return adv.at[:, pl.ds(pl.multiple_of(r * 512 + lo * 256 + c * 128, 128), 128)]

    def scatter(c):
        def send(i, carry):
            to = lax.rem(me + i, 2 * MEMBERS)
            to_lo, to_r = to // MEMBERS, to % MEMBERS
            start = pl.multiple_of(to_r * 512 + to_lo * 256 + c * 128, 128)
            remote(
                adv.at[:, pl.ds(start, 128)], ext.at[c, 16 + me],
                send_sem.at[6 + c], recv_sem.at[7 + c], 2 * y + to_lo, to_r,
            ).start()
            return carry

        lax.fori_loop(1, 2 * MEMBERS, send, 0)
        pltpu.make_async_copy(my_columns(c), ext.at[c, 16 + me], recv_sem.at[7 + c]).start()

    scatter(0)

    ut = pltpu.roll(u12.T, lax.rem(2 * NX - 16 * y + 2, NX), 1)
    vt = pltpu.roll(v12.T, lax.rem(2 * NX - 16 * y + 2, NX), 1)
    for k in range(20):
        ub[k] = jnp.broadcast_to(ut[:, k : k + 1], (NX, NX))
        vb[k] = jnp.broadcast_to(vt[:, k : k + 1], (NX, NX))

    @pl.when(g == 0)
    def _():
        pieces[0:16] = jnp.zeros((16, 8, NX), f32)

    @pl.when(g == GROUPS - 1)
    def _():
        pieces[48:64] = jnp.zeros((16, 8, NX), f32)

    @pl.when(y == 0)
    def _():
        for c in range(2):
            ext[c, 0:16] = jnp.zeros((16, ROWS, NX), f32)

    @pl.when(y == 7)
    def _():
        for c in range(2):
            ext[c, 80:96] = jnp.zeros((16, ROWS, NX), f32)

    drain(pieces.at[16:48], recv_sem.at[0])

    @pl.when(g > 0)
    def _():
        drain(pieces.at[0:16], recv_sem.at[1])

    @pl.when(g < GROUPS - 1)
    def _():
        drain(pieces.at[48:64], recv_sem.at[2])

    for k in range(16):
        near[:, k * NX : (k + 1) * NX] = (
            pieces[4 * k] + pieces[4 * k + 1] + pieces[4 * k + 2] + pieces[4 * k + 3]
        )

    def at(ref, k):
        return ref[:, k * NX : (k + 1) * NX]

    def near_slope(ref, k):
        return lane_slope(
            factors_at(8 * g + k), at(ref, k), at(ref, k + 1), at(ref, k - 1),
            at(ref, k + 2), at(ref, k - 2),
        )

    for k in range(2, 14):
        mid8[:, k * NX : (k + 1) * NX] = at(near, k) + near_slope(near, k)
    for k in range(4, 12):
        yt[:, (k - 4) * NX : (k - 3) * NX] = 0.5 * (at(near, k) + at(mid8, k) + near_slope(mid8, k))

    cell_at = lax.broadcasted_iota(jnp.int32, (1024, OBS), 0)
    chosen = jnp.where(cell_at == obs_row_ref[...] - 1024 * g, 1.0, 0.0)
    spart[...] = dot(yt[...], chosen)
    sparts[g] = spart[...]

    def to_groups(i, carry):
        to = lax.rem(g + i, GROUPS)
        remote(spart, sparts.at[g], send_sem.at[2], recv_sem.at[3], to, r).start()
        return carry

    lax.fori_loop(1, GROUPS, to_groups, 0)

    @pl.when(on_diagonal)
    def _():
        pltpu.make_async_copy(yt, rt, recv_sem.at[5]).start()

    @pl.when(jnp.logical_not(on_diagonal))
    def _():
        remote(yt, rt, send_sem.at[4], recv_sem.at[5], chip, 2 * g + core).start()

    yg[chip, core] = yt[...]

    def to_group(i, carry):
        to = lax.rem(r + 2 * i, MEMBERS)
        remote(yt, yg.at[chip, core], send_sem.at[5], recv_sem.at[6], g, to).start()
        return carry

    lax.fori_loop(1, GROUPS, to_group, 0)
    drain(sparts.at[0:15], recv_sem.at[3])
    srow[...] = jnp.sum(sparts[...], axis=0)
    s_all[r] = srow[...]

    def block_row(i, carry):
        to = lax.rem(r + i, MEMBERS)
        remote(srow, s_all.at[r], send_sem.at[3], recv_sem.at[4], g, to).start()
        return carry

    lax.fori_loop(1, MEMBERS, block_row, 0)

    drain(rt, recv_sem.at[5])

    def to_columns(i, carry):
        grp = lax.rem(g + i // 2, GROUPS)
        half = lax.rem(core + i, 2)
        remote(
            rt.at[:, pl.ds(pl.multiple_of(half * 512, 512), 512)], yr.at[2 * g + core],
            send_sem.at[8], recv_sem.at[9], grp, 2 * chip + half,
        ).start()
        return carry

    lax.fori_loop(1, 2 * GROUPS, to_columns, 0)
    pltpu.make_async_copy(
        rt.at[:, pl.ds(pl.multiple_of(core * 512, 512), 512)], yr.at[2 * g + core], recv_sem.at[9]
    ).start()
    scatter(1)

    drain(s_all.at[0:31], recv_sem.at[4])
    diagonal = lax.broadcasted_iota(jnp.int32, (128, 128), 0) == lax.broadcasted_iota(
        jnp.int32, (128, 128), 1
    )
    s11 = s_all[0:16, :, 0:128].reshape(128, 128)
    first[...] = 0.5 * (s11 + s11.T) + jnp.where(diagonal, var_ref[0:1, :], 0.0)
    negative_inverse(first)

    drain(yg.at[0:15, 0], recv_sem.at[6])
    relay = remote(
        yg.at[:, core], yg.at[:, core], send_sem.at[9], recv_sem.at[10], g, 2 * chip + 1 - core
    )
    relay.start()

    def up(c):
        return remote(
            ext.at[c, 64:80], ext.at[c, 0:16], send_sem.at[10 + c], recv_sem.at[11 + c], g + 2, r
        )

    def down(c):
        return remote(
            ext.at[c, 16:32], ext.at[c, 80:96], send_sem.at[12 + c], recv_sem.at[13 + c], g - 2, r
        )

    def trade(c):
        return remote(
            fore.at[c, 1 - lo], theirs.at[c], send_sem.at[14 + c], recv_sem.at[15 + c],
            2 * y + 1 - lo, r,
        )

    def start_halo(c):
        drain(ext.at[c, 16:80], recv_sem.at[7 + c])

        @pl.when(y < 7)
        def _():
            up(c).start()

        @pl.when(y > 0)
        def _():
            down(c).start()

    start_halo(0)

    s12 = s_all[0:16, :, 128:256].reshape(128, 128)
    s21 = s_all[16:32, :, 0:128].reshape(128, 128)
    s22 = s_all[16:32, :, 128:256].reshape(128, 128)
    inner = s22 + dot(s21, dot(first[...], s12))
    second[...] = 0.5 * (inner + inner.T) + jnp.where(diagonal, var_ref[1:2, :], 0.0)
    negative_inverse(second)
    drain(yr, recv_sem.at[9])
    r1 = yr[0:16].reshape(128, 512)
    r2 = yr[16:32].reshape(128, 512)
    z2 = -dot(second[...], r2 + dot(s21, dot(first[...], r1)))
    z1 = -dot(first[...], r1 - dot(s12, z2))
    for k, z in ((0, z1), (1, z2)):
        high = z.astype(bf16)
        zh[k * 128 : (k + 1) * 128, :] = high
        zl[k * 128 : (k + 1) * 128, :] = (z - high.astype(f32)).astype(bf16)
    relay.wait_recv()
    for j in range(8):
        q = yg[:, :, :, j * NX : (j + 1) * NX].reshape(OBS, NX).T
        high = q.astype(bf16)
        qh[j] = high
        ql[j] = (q - high.astype(f32)).astype(bf16)

    def grid_row(c, k):
        return jnp.concatenate([ext[c, 4 * k + i] for i in range(4)], axis=0)

    def column_first(c, start, stop):
        def step(k, carry):
            q = grid_row(c, k)
            inside = (y * 16 + k - 4 >= 0) & (y * 16 + k - 4 < NY)
            slope = column_slope(
                q, grid_row(c, k + 1), grid_row(c, k - 1), grid_row(c, k + 2), grid_row(c, k - 2),
                ub[k - 2], vb[k - 2],
            )
            mid[k - 2] = jnp.where(inside, q + slope, 0.0)
            return carry

        lax.fori_loop(start, stop, step, 0)

    def column_second(c, half):
        def step(j, carry):
            k = half * 8 + j + 4
            q = mid[k - 2]
            slope = column_slope(
                q, mid[k - 1], mid[k - 3], mid[k], mid[k - 4], ub[k - 2], vb[k - 2]
            )
            fore[c, half, j] = 0.5 * (grid_row(c, k) + q + slope)
            return carry

        lax.fori_loop(0, 8, step, 0)

    def correct(column, field):
        cols = pl.ds(pl.multiple_of(column, 128), 128)
        b_high, b_low = zh[:, cols], zl[:, cols]

        def part(a, b):
            return jnp.dot(a, b, preferred_element_type=f32)

        def step(j, carry):
            a_high, a_low = qh[j], ql[j]
            out_ref[pl.ds(pl.multiple_of(j * NX, NX), NX), cols] = field(j) - (
                part(a_high, b_high) + part(a_high, b_low) + part(a_low, b_high)
            )
            return carry

        lax.fori_loop(0, 8, step, 0)

    for c in range(2):
        if c == 1:
            start_halo(1)
        column_first(c, 6, 18)

        @pl.when(y > 0)
        def _():
            up(c).wait_recv()

        @pl.when(y < 7)
        def _():
            down(c).wait_recv()

        column_first(c, 2, 6)
        column_first(c, 18, 22)
        column_second(c, 1 - lo)
        trade(c).start()
        column_second(c, lo)
        correct(lo * 256 + c * 128, lambda j: fore[c, lo, j])
    for c in range(2):
        trade(c).wait_recv()
        correct((1 - lo) * 256 + c * 128, lambda j: theirs[c, j])

    drain(pieces.at[0:31], send_sem.at[0])

    @pl.when(has_side)
    def _():
        drain(pieces.at[0:32], send_sem.at[1])

    drain(sparts.at[0:15], send_sem.at[2])
    drain(s_all.at[0:31], send_sem.at[3])

    @pl.when(jnp.logical_not(on_diagonal))
    def _():
        drain(rt, send_sem.at[4])

    drain(yg.at[0:15, 0], send_sem.at[5])
    drain(yr.at[0:31], send_sem.at[8])
    relay.wait_send()
    for c in range(2):
        drain(ext.at[c, 0:63], send_sem.at[6 + c])
        trade(c).wait_send()

        @pl.when(y < 7)
        def _():
            up(c).wait_send()

        @pl.when(y > 0)
        def _():
            down(c).wait_send()


def local(cov_prior, courant_x_field, courant_y_field, obs_cells, obs_var):
    f32, bf16 = jnp.float32, jnp.bfloat16
    scratch = [
        ((8, 136, NX), f32),
        ((ROWS, NCELL), f32),
        ((ROWS, NCELL), f32),
        ((OBS, NX), f32),
        ((64, 8, NX), f32),
        ((8, 2048), f32),
        ((8, 2048), f32),
        ((8, 1024), f32),
        ((8, 1024), f32),
        ((8, OBS), f32),
        ((GROUPS, 8, OBS), f32),
        ((8, OBS), f32),
        ((MEMBERS, 8, OBS), f32),
        ((GROUPS, 2, 8, 1024), f32),
        ((MEMBERS, 8, 512), f32),
        ((128, 128), f32),
        ((128, 128), f32),
        ((2, 96, ROWS, NX), f32),
        ((20, NX, NX), f32),
        ((2, 2, 8, NX, NX), f32),
        ((2, 8, NX, NX), f32),
        ((20, NX, NX), f32),
        ((20, NX, NX), f32),
        ((8, NX, OBS), bf16),
        ((8, NX, OBS), bf16),
        ((OBS, 512), bf16),
        ((OBS, 512), bf16),
    ]
    return pl.pallas_call(
        kernel,
        out_shape=jax.ShapeDtypeStruct((1024, 512), f32),
        in_specs=[VMEM] * 5,
        out_specs=VMEM,
        scratch_shapes=[pltpu.VMEM(shape, dtype) for shape, dtype in scratch]
        + [pltpu.SemaphoreType.DMA((16,)), pltpu.SemaphoreType.DMA((17,))],
        compiler_params=pltpu.CompilerParams(
            collective_id=0, has_side_effects=True, vmem_limit_bytes=VMEM_LIMIT
        ),
    )(obs_cells.reshape(1, OBS), cov_prior, courant_x_field, courant_y_field, obs_var)


def solution(mesh):
    placed = (P(("grp", "row"), None), P(), P(), P(), P())
    return jax.shard_map(
        local, mesh=mesh, in_specs=placed, out_specs=P("grp", "row"), check_vma=False
    )
```

```python
import jax
import jax.numpy as jnp
from jax import lax
from jax.experimental import pallas as pl
from jax.experimental.pallas import tpu as pltpu
from jax.sharding import PartitionSpec as P

NX = 128
NY = 128
NCELL = NX * NY
OBS = 256
GROUPS = 16
MEMBERS = 32
ROWS = 32
HIGHEST = lax.Precision.HIGHEST
MESH = pl.DeviceIdType.MESH
VMEM = pl.BlockSpec(memory_space=pltpu.VMEM)
FIRST_BATCH = 40
SECOND_BATCH = 64
STRIDE = 27
VMEM_LIMIT = 48 * 1024 * 1024


def lane_slope(cf, q, yp1, ym1, yp2, ym2):
    return (
        cf[0] * pltpu.roll(q, NX - 1, 1)
        + cf[1] * pltpu.roll(q, 1, 1)
        + cf[2] * pltpu.roll(q, NX - 2, 1)
        + cf[3] * pltpu.roll(q, 2, 1)
        + cf[4] * yp1
        + cf[5] * ym1
        + cf[6] * yp2
        + cf[7] * ym2
        - 0.4 * q
    )


def lanes(y):
    return pl.ds(pl.multiple_of(y * NX, NX), NX)


def drain(ref, sem):
    pltpu.make_async_copy(ref, ref, sem).wait()


def remote(src, dst, send_sem, recv_sem, grp, row):
    return pltpu.make_async_remote_copy(
        src_ref=src,
        dst_ref=dst,
        send_sem=send_sem,
        recv_sem=recv_sem,
        device_id={"grp": grp, "row": row},
        device_id_type=MESH,
    )


PIVOTS = 4


def negative_inverse(ref):
    lane = lax.broadcasted_iota(jnp.int32, (1, 128), 1)
    some = range(PIVOTS)

    def step(h, carry):
        k = pl.multiple_of(h * PIVOTS, PIVOTS)
        at = [lane == k + m for m in some]
        rows = [ref[pl.ds(k + m, 1), :] for m in some]
        a = ref[...]

        def column(m, of):
            return jnp.sum(jnp.where(at[m], of, 0.0), axis=1, keepdims=True)

        cols = [column(m, a) for m in some]
        block = [[column(max(i, j), rows[min(i, j)]) for j in some] for i in some]
        for m in some:
            inv = 1.0 / block[m][m]
            scaled = [block[m][j] * inv for j in some]
            swept = [[None] * PIVOTS for _ in some]
            for i in some:
                for j in range(i, PIVOTS):
                    if i == m and j == m:
                        value = -inv
                    elif i == m:
                        value = scaled[j]
                    elif j == m:
                        value = scaled[i]
                    else:
                        value = block[i][j] - block[i][m] * scaled[j]
                    swept[i][j] = swept[j][i] = value
            block = swept
        new = jnp.where((lane >= k) & (lane < k + PIVOTS), 0.0, a)
        new_rows = []
        for m in some:
            row = -block[m][0] * rows[0]
            for j in range(1, PIVOTS):
                row = row - block[m][j] * rows[j]
            for j in some:
                row = jnp.where(at[j], block[m][j], row)
            new_rows.append(row)
            new = new - cols[m] * row
        ref[...] = new
        for m in some:
            ref[pl.ds(k + m, 1), :] = new_rows[m]
        return carry

    lax.fori_loop(0, 128 // PIVOTS, step, 0)


def dot(a, b):
    return jnp.dot(a, b, precision=HIGHEST, preferred_element_type=jnp.float32)


def dot(a, b):
    return jnp.dot(a, b, precision=HIGHEST, preferred_element_type=jnp.float32)


def column_slope(q, yp1, ym1, yp2, ym2, u12, v12):
    x = lax.broadcasted_iota(jnp.int32, (NX, NX), 0)
    xp1 = jnp.where(x < NX - 1, pltpu.roll(q, NX - 1, 0), 0.0)
    xm1 = jnp.where(x > 0, pltpu.roll(q, 1, 0), 0.0)
    xp2 = jnp.where(x < NX - 2, pltpu.roll(q, NX - 2, 0), 0.0)
    xm2 = jnp.where(x > 1, pltpu.roll(q, 2, 0), 0.0)
    along_x = 8.0 * (xp1 - xm1) - (xp2 - xm2)
    along_y = 8.0 * (yp1 - ym1) - (yp2 - ym2)
    laplace = xp1 + xm1 + yp1 + ym1 - 4.0 * q
    return 0.1 * laplace - u12 * along_x - v12 * along_y


def kernel(
    obs_row_ref, c_ref, u_ref, v_ref, var_ref, out_ref,
    coef, q1, adv, aot, pieces, near, mid8, yt, rt, spart, sparts, srow, s_all, yg, yr, first, second,
    ext, mid, fore, theirs, ub, vb, qh, ql, zh, zl, send_sem, recv_sem,
):
    f32, bf16 = jnp.float32, jnp.bfloat16
    g = lax.axis_index("grp")
    r = lax.axis_index("row")
    y, lo = g // 2, g % 2
    chip, core = r // 2, r % 2
    me = lo * MEMBERS + r

    barrier = pltpu.get_barrier_semaphore()

    def greet(grp, row):
        pl.semaphore_signal(
            barrier, inc=1, device_id={"grp": grp, "row": row}, device_id_type=MESH
        )

    def greet_plane(i, carry):
        to = lax.rem(me + i, 2 * MEMBERS)
        greet(2 * y + to // MEMBERS, to % MEMBERS)
        return carry

    lax.fori_loop(1, 2 * MEMBERS, greet_plane, 0)
    across = jnp.where(lo == 0, g - 1, g + 1)
    has_across = (across >= 0) & (across < GROUPS)

    @pl.when(has_across)
    def _():
        def greet_across(i, carry):
            greet(across, i)
            return carry

        lax.fori_loop(0, MEMBERS, greet_across, 0)

    def greet_planes(i, carry):
        greet(lax.rem(2 * y + 2 + i // 2, GROUPS), 2 * chip + i % 2)
        return carry

    lax.fori_loop(0, 2 * GROUPS - 4, greet_planes, 0)
    on_diagonal = chip == g

    @pl.when(jnp.logical_not(on_diagonal))
    def _():
        greet(chip, 2 * g + core)

    gx = lax.broadcasted_iota(jnp.int32, (NY, NX), 1)
    gy = lax.broadcasted_iota(jnp.int32, (NY, NX), 0)
    u12 = u_ref[...] * (1.0 / 12.0)
    v12 = v_ref[...] * (1.0 / 12.0)
    factors = (
        jnp.where(gx < NX - 1, 0.1 - 8.0 * u12, 0.0),
        jnp.where(gx > 0, 0.1 + 8.0 * u12, 0.0),
        jnp.where(gx < NX - 2, u12, 0.0),
        jnp.where(gx > 1, -u12, 0.0),
        jnp.where(gy < NY - 1, 0.1 - 8.0 * v12, 0.0),
        jnp.where(gy > 0, 0.1 + 8.0 * v12, 0.0),
        jnp.where(gy < NY - 2, v12, 0.0),
        jnp.where(gy > 1, -v12, 0.0),
    )
    for k in range(8):
        coef[k, 0:8] = jnp.zeros((8, NX), f32)
        coef[k, 128:136] = jnp.zeros((8, NX), f32)
        coef[k, 4 : 4 + NY] = factors[k]

    def factors_at(row):
        return [coef[k, pl.ds(row, 1), :] for k in range(8)]

    def read(ref, yy):
        return ref[:, lanes(jnp.clip(yy, 0, NY - 1))]

    def row_slope(ref, yy):
        return lane_slope(
            factors_at(yy + 4), read(ref, yy), read(ref, yy + 1), read(ref, yy - 1),
            read(ref, yy + 2), read(ref, yy - 2),
        )

    def row_first(yy, carry):
        q1[:, lanes(yy)] = c_ref[:, lanes(yy)] + row_slope(c_ref, yy)
        return carry

    cells = obs_row_ref[...]
    chosen_x = jnp.where(
        lax.broadcasted_iota(jnp.int32, (NX, OBS), 0) == cells % NX, 1.0, 0.0
    ).astype(bf16)
    cells_y = cells // NX

    def row_second(yy, acc):
        new = 0.5 * (c_ref[:, lanes(yy)] + q1[:, lanes(yy)] + row_slope(q1, yy))
        adv[:, lanes(yy)] = new
        high = new.astype(bf16)
        rest = new - high.astype(f32)
        middle = rest.astype(bf16)
        low = (rest - middle.astype(f32)).astype(bf16)
        parts = jnp.dot(
            jnp.concatenate([high, middle, low], axis=0), chosen_x, preferred_element_type=f32
        )
        found = parts[0:ROWS] + (parts[ROWS : 2 * ROWS] + parts[2 * ROWS :])
        return jnp.where(cells_y == yy, found, acc)

    lax.fori_loop(0, NY, row_first, 0, unroll=4)
    acc = lax.fori_loop(0, NY, row_second, jnp.zeros((ROWS, OBS), f32), unroll=4)

    quarter = r % 4
    place = lax.broadcasted_iota(jnp.int32, (NX, NX), 0) // ROWS == quarter
    for update in range(2):
        part = acc[:, update * NX : (update + 1) * NX]
        full = jnp.where(place, jnp.concatenate([part] * 4, axis=0), 0.0)
        aot[update * NX : (update + 1) * NX, :] = full.T

    pl.semaphore_wait(
        barrier,
        2 * MEMBERS - 1 + 2 * GROUPS - 4
        + jnp.where(has_across, MEMBERS, 0) + jnp.where(on_diagonal, 0, 1),
    )

    def some(to):
        return aot.at[pl.ds(pl.multiple_of(to * 8, 8), 8)]

    def share(i, carry):
        to = lax.rem(r + i, MEMBERS)
        remote(some(to), pieces.at[16 + r], send_sem.at[0], recv_sem.at[0], g, to).start()
        return carry

    lax.fori_loop(1, MEMBERS, share, 0)
    pltpu.make_async_copy(some(r), pieces.at[16 + r], recv_sem.at[0]).start()
    y_in = r // 4
    low = y_in < 4
    side = jnp.where(low, g - 1, g + 1)
    slot = jnp.where(low, 12 + y_in, y_in - 4) * 4 + quarter
    has_side = (side >= 0) & (side < GROUPS)

    @pl.when(has_side)
    def _():
        def share_side(i, carry):
            to = lax.rem(r + i, MEMBERS)
            remote(
                some(to), pieces.at[slot], send_sem.at[1], recv_sem.at[jnp.where(low, 2, 1)], side, to
            ).start()
            return carry

        lax.fori_loop(0, MEMBERS, share_side, 0)

    def my_columns(c):
        return adv.at[:, pl.ds(pl.multiple_of(r * 512 + lo * 256 + c * 128, 128), 128)]

    def scatter(c, start, stop):
        def send(i, carry):
            to = lax.rem(me + STRIDE * i, 2 * MEMBERS)
            to_lo, to_r = to // MEMBERS, to % MEMBERS
            column = pl.multiple_of(to_r * 512 + to_lo * 256 + c * 128, 128)
            remote(
                adv.at[:, pl.ds(column, 128)], ext.at[c, 16 + me],
                send_sem.at[6 + c], recv_sem.at[7 + c], 2 * y + to_lo, to_r,
            ).start()
            return carry

        lax.fori_loop(start, stop, send, 0)

    for c in range(2):
        pltpu.make_async_copy(my_columns(c), ext.at[c, 16 + me], recv_sem.at[7 + c]).start()
    scatter(0, 1, FIRST_BATCH)

    ut = pltpu.roll(u12.T, lax.rem(2 * NX - 16 * y + 2, NX), 1)
    vt = pltpu.roll(v12.T, lax.rem(2 * NX - 16 * y + 2, NX), 1)
    for k in range(20):
        ub[k] = jnp.broadcast_to(ut[:, k : k + 1], (NX, NX))
        vb[k] = jnp.broadcast_to(vt[:, k : k + 1], (NX, NX))

    @pl.when(g == 0)
    def _():
        pieces[0:16] = jnp.zeros((16, 8, NX), f32)

    @pl.when(g == GROUPS - 1)
    def _():
        pieces[48:64] = jnp.zeros((16, 8, NX), f32)

    @pl.when(y == 0)
    def _():
        for c in range(2):
            ext[c, 0:16] = jnp.zeros((16, ROWS, NX), f32)

    @pl.when(y == 7)
    def _():
        for c in range(2):
            ext[c, 80:96] = jnp.zeros((16, ROWS, NX), f32)

    drain(pieces.at[16:48], recv_sem.at[0])

    @pl.when(g > 0)
    def _():
        drain(pieces.at[0:16], recv_sem.at[1])

    @pl.when(g < GROUPS - 1)
    def _():
        drain(pieces.at[48:64], recv_sem.at[2])

    for k in range(16):
        near[:, k * NX : (k + 1) * NX] = (
            pieces[4 * k] + pieces[4 * k + 1] + pieces[4 * k + 2] + pieces[4 * k + 3]
        )

    def at(ref, k):
        return ref[:, k * NX : (k + 1) * NX]

    def near_slope(ref, k):
        return lane_slope(
            factors_at(8 * g + k), at(ref, k), at(ref, k + 1), at(ref, k - 1),
            at(ref, k + 2), at(ref, k - 2),
        )

    for k in range(2, 14):
        mid8[:, k * NX : (k + 1) * NX] = at(near, k) + near_slope(near, k)
    for k in range(4, 12):
        yt[:, (k - 4) * NX : (k - 3) * NX] = 0.5 * (at(near, k) + at(mid8, k) + near_slope(mid8, k))

    cell_at = lax.broadcasted_iota(jnp.int32, (1024, OBS), 0)
    chosen = jnp.where(cell_at == obs_row_ref[...] - 1024 * g, 1.0, 0.0)
    spart[...] = dot(yt[...], chosen)
    sparts[g] = spart[...]

    def to_groups(i, carry):
        to = lax.rem(g + i, GROUPS)
        remote(spart, sparts.at[g], send_sem.at[2], recv_sem.at[3], to, r).start()
        return carry

    lax.fori_loop(1, GROUPS, to_groups, 0)

    @pl.when(on_diagonal)
    def _():
        pltpu.make_async_copy(yt, rt, recv_sem.at[5]).start()

    @pl.when(jnp.logical_not(on_diagonal))
    def _():
        remote(yt, rt, send_sem.at[4], recv_sem.at[5], chip, 2 * g + core).start()

    yg[chip, core] = yt[...]
    scatter(0, FIRST_BATCH, SECOND_BATCH)
    drain(sparts.at[0:15], recv_sem.at[3])
    srow[...] = jnp.sum(sparts[...], axis=0)
    s_all[r] = srow[...]

    def block_row(i, carry):
        to = lax.rem(r + i, MEMBERS)
        remote(srow, s_all.at[r], send_sem.at[3], recv_sem.at[4], g, to).start()
        return carry

    lax.fori_loop(1, MEMBERS, block_row, 0)

    drain(rt, recv_sem.at[5])

    def to_columns(i, carry):
        grp = lax.rem(g + i // 2, GROUPS)
        half = lax.rem(core + i, 2)
        remote(
            rt.at[:, pl.ds(pl.multiple_of(half * 512, 512), 512)], yr.at[2 * g + core],
            send_sem.at[8], recv_sem.at[9], grp, 2 * chip + half,
        ).start()
        return carry

    lax.fori_loop(1, 2 * GROUPS, to_columns, 0)
    pltpu.make_async_copy(
        rt.at[:, pl.ds(pl.multiple_of(core * 512, 512), 512)], yr.at[2 * g + core], recv_sem.at[9]
    ).start()

    scatter(0, SECOND_BATCH, 2 * MEMBERS)
    scatter(1, 1, 2 * MEMBERS)

    def to_group(i, carry):
        to = lax.rem(r + 2 * i, MEMBERS)
        remote(yt, yg.at[chip, core], send_sem.at[5], recv_sem.at[6], g, to).start()
        return carry

    lax.fori_loop(1, GROUPS, to_group, 0)

    drain(s_all.at[0:31], recv_sem.at[4])
    diagonal = lax.broadcasted_iota(jnp.int32, (128, 128), 0) == lax.broadcasted_iota(
        jnp.int32, (128, 128), 1
    )
    s11 = s_all[0:16, :, 0:128].reshape(128, 128)
    first[...] = 0.5 * (s11 + s11.T) + jnp.where(diagonal, var_ref[0:1, :], 0.0)
    negative_inverse(first)

    relay = remote(
        yg.at[:, core], yg.at[:, core], send_sem.at[9], recv_sem.at[10], g, 2 * chip + 1 - core
    )

    def up(c):
        return remote(
            ext.at[c, 64:80], ext.at[c, 0:16], send_sem.at[10 + c], recv_sem.at[11 + c], g + 2, r
        )

    def down(c):
        return remote(
            ext.at[c, 16:32], ext.at[c, 80:96], send_sem.at[12 + c], recv_sem.at[13 + c], g - 2, r
        )

    def trade(c):
        return remote(
            fore.at[c, 1 - lo], theirs.at[c], send_sem.at[14 + c], recv_sem.at[15 + c],
            2 * y + 1 - lo, r,
        )

    def start_halo(c):
        drain(ext.at[c, 16:80], recv_sem.at[7 + c])

        @pl.when(y < 7)
        def _():
            up(c).start()

        @pl.when(y > 0)
        def _():
            down(c).start()

    start_halo(0)

    s12 = s_all[0:16, :, 128:256].reshape(128, 128)
    s21 = s_all[16:32, :, 0:128].reshape(128, 128)
    s22 = s_all[16:32, :, 128:256].reshape(128, 128)
    inner = s22 + dot(s21, dot(first[...], s12))
    second[...] = 0.5 * (inner + inner.T) + jnp.where(diagonal, var_ref[1:2, :], 0.0)
    negative_inverse(second)
    def grid_row(c, k):
        return jnp.concatenate([ext[c, 4 * k + i] for i in range(4)], axis=0)

    def column_first(c, start, stop):
        def step(k, carry):
            q = grid_row(c, k)
            inside = (y * 16 + k - 4 >= 0) & (y * 16 + k - 4 < NY)
            slope = column_slope(
                q, grid_row(c, k + 1), grid_row(c, k - 1), grid_row(c, k + 2), grid_row(c, k - 2),
                ub[k - 2], vb[k - 2],
            )
            mid[k - 2] = jnp.where(inside, q + slope, 0.0)
            return carry

        lax.fori_loop(start, stop, step, 0)

    def column_second(c, half):
        def step(j, carry):
            k = half * 8 + j + 4
            q = mid[k - 2]
            slope = column_slope(
                q, mid[k - 1], mid[k - 3], mid[k], mid[k - 4], ub[k - 2], vb[k - 2]
            )
            fore[c, half, j] = 0.5 * (grid_row(c, k) + q + slope)
            return carry

        lax.fori_loop(0, 8, step, 0)

    def correct(column, field):
        cols = pl.ds(pl.multiple_of(column, 128), 128)
        b_high, b_low = zh[:, cols], zl[:, cols]

        def part(a, b):
            return jnp.dot(a, b, preferred_element_type=f32)

        def step(j, carry):
            a_high, a_low = qh[j], ql[j]
            out_ref[pl.ds(pl.multiple_of(j * NX, NX), NX), cols] = field(j) - (
                part(a_high, b_high) + part(a_high, b_low) + part(a_low, b_high)
            )
            return carry

        lax.fori_loop(0, 8, step, 0)

    for c in range(2):
        if c == 1:
            start_halo(1)
        column_first(c, 6, 18)
        if c == 1:
            drain(yg.at[0:15, 0], recv_sem.at[6])
            relay.start()

        @pl.when(y > 0)
        def _():
            up(c).wait_recv()

        @pl.when(y < 7)
        def _():
            down(c).wait_recv()

        column_first(c, 2, 6)
        column_first(c, 18, 22)
        column_second(c, 1 - lo)
        trade(c).start()
        column_second(c, lo)

    drain(yr, recv_sem.at[9])
    r1 = yr[0:16].reshape(128, 512)
    r2 = yr[16:32].reshape(128, 512)
    z2 = -dot(second[...], r2 + dot(s21, dot(first[...], r1)))
    z1 = -dot(first[...], r1 - dot(s12, z2))
    for k, z in ((0, z1), (1, z2)):
        high = z.astype(bf16)
        zh[k * 128 : (k + 1) * 128, :] = high
        zl[k * 128 : (k + 1) * 128, :] = (z - high.astype(f32)).astype(bf16)
    relay.wait_recv()
    for j in range(8):
        q = yg[:, :, :, j * NX : (j + 1) * NX].reshape(OBS, NX).T
        high = q.astype(bf16)
        qh[j] = high
        ql[j] = (q - high.astype(f32)).astype(bf16)
    for c in range(2):
        correct(lo * 256 + c * 128, lambda j: fore[c, lo, j])
    for c in range(2):
        trade(c).wait_recv()
        correct((1 - lo) * 256 + c * 128, lambda j: theirs[c, j])

    drain(pieces.at[0:31], send_sem.at[0])

    @pl.when(has_side)
    def _():
        drain(pieces.at[0:32], send_sem.at[1])

    drain(sparts.at[0:15], send_sem.at[2])
    drain(s_all.at[0:31], send_sem.at[3])

    @pl.when(jnp.logical_not(on_diagonal))
    def _():
        drain(rt, send_sem.at[4])

    drain(yg.at[0:15, 0], send_sem.at[5])
    drain(yr.at[0:31], send_sem.at[8])
    relay.wait_send()
    for c in range(2):
        drain(ext.at[c, 0:63], send_sem.at[6 + c])
        trade(c).wait_send()

        @pl.when(y < 7)
        def _():
            up(c).wait_send()

        @pl.when(y > 0)
        def _():
            down(c).wait_send()


def local(cov_prior, courant_x_field, courant_y_field, obs_cells, obs_var):
    f32, bf16 = jnp.float32, jnp.bfloat16
    scratch = [
        ((8, 136, NX), f32),
        ((ROWS, NCELL), f32),
        ((ROWS, NCELL), f32),
        ((OBS, NX), f32),
        ((64, 8, NX), f32),
        ((8, 2048), f32),
        ((8, 2048), f32),
        ((8, 1024), f32),
        ((8, 1024), f32),
        ((8, OBS), f32),
        ((GROUPS, 8, OBS), f32),
        ((8, OBS), f32),
        ((MEMBERS, 8, OBS), f32),
        ((GROUPS, 2, 8, 1024), f32),
        ((MEMBERS, 8, 512), f32),
        ((128, 128), f32),
        ((128, 128), f32),
        ((2, 96, ROWS, NX), f32),
        ((20, NX, NX), f32),
        ((2, 2, 8, NX, NX), f32),
        ((2, 8, NX, NX), f32),
        ((20, NX, NX), f32),
        ((20, NX, NX), f32),
        ((8, NX, OBS), bf16),
        ((8, NX, OBS), bf16),
        ((OBS, 512), bf16),
        ((OBS, 512), bf16),
    ]
    return pl.pallas_call(
        kernel,
        out_shape=jax.ShapeDtypeStruct((1024, 512), f32),
        in_specs=[VMEM] * 5,
        out_specs=VMEM,
        scratch_shapes=[pltpu.VMEM(shape, dtype) for shape, dtype in scratch]
        + [pltpu.SemaphoreType.DMA((16,)), pltpu.SemaphoreType.DMA((17,))],
        compiler_params=pltpu.CompilerParams(
            collective_id=0, has_side_effects=True, vmem_limit_bytes=VMEM_LIMIT
        ),
    )(obs_cells.reshape(1, OBS), cov_prior, courant_x_field, courant_y_field, obs_var)


def solution(mesh):
    placed = (P(("grp", "row"), None), P(), P(), P(), P())
    return jax.shard_map(
        local, mesh=mesh, in_specs=placed, out_specs=P("grp", "row"), check_vma=False
    )
```

```python
import jax
import jax.numpy as jnp
from jax import lax
from jax.experimental import pallas as pl
from jax.experimental.pallas import tpu as pltpu
from jax.sharding import PartitionSpec as P

NX = 128
NY = 128
NCELL = NX * NY
OBS = 256
GROUPS = 16
MEMBERS = 32
ROWS = 32
HIGHEST = lax.Precision.HIGHEST
MESH = pl.DeviceIdType.MESH
VMEM = pl.BlockSpec(memory_space=pltpu.VMEM)
FIRST_BATCH = 40
SECOND_BATCH = 64
EARLY = 1
STRIDE = 27
VMEM_LIMIT = 62 * 1024 * 1024


def lane_slope(cf, q, yp1, ym1, yp2, ym2):
    return (
        cf[0] * pltpu.roll(q, NX - 1, 1)
        + cf[1] * pltpu.roll(q, 1, 1)
        + cf[2] * pltpu.roll(q, NX - 2, 1)
        + cf[3] * pltpu.roll(q, 2, 1)
        + cf[4] * yp1
        + cf[5] * ym1
        + cf[6] * yp2
        + cf[7] * ym2
        - 0.4 * q
    )


def lanes(y):
    return pl.ds(pl.multiple_of(y * NX, NX), NX)


def drain(ref, sem):
    pltpu.make_async_copy(ref, ref, sem).wait()


def remote(src, dst, send_sem, recv_sem, grp, row):
    return pltpu.make_async_remote_copy(
        src_ref=src,
        dst_ref=dst,
        send_sem=send_sem,
        recv_sem=recv_sem,
        device_id={"grp": grp, "row": row},
        device_id_type=MESH,
    )


PIVOTS = 4


def negative_inverse(ref):
    lane = lax.broadcasted_iota(jnp.int32, (1, 128), 1)
    some = range(PIVOTS)

    def step(h, carry):
        k = pl.multiple_of(h * PIVOTS, PIVOTS)
        at = [lane == k + m for m in some]
        rows = [ref[pl.ds(k + m, 1), :] for m in some]
        a = ref[...]

        def column(m, of):
            return jnp.sum(jnp.where(at[m], of, 0.0), axis=1, keepdims=True)

        cols = [column(m, a) for m in some]
        block = [[column(max(i, j), rows[min(i, j)]) for j in some] for i in some]
        for m in some:
            inv = 1.0 / block[m][m]
            scaled = [block[m][j] * inv for j in some]
            swept = [[None] * PIVOTS for _ in some]
            for i in some:
                for j in range(i, PIVOTS):
                    if i == m and j == m:
                        value = -inv
                    elif i == m:
                        value = scaled[j]
                    elif j == m:
                        value = scaled[i]
                    else:
                        value = block[i][j] - block[i][m] * scaled[j]
                    swept[i][j] = swept[j][i] = value
            block = swept
        new = jnp.where((lane >= k) & (lane < k + PIVOTS), 0.0, a)
        new_rows = []
        for m in some:
            row = -block[m][0] * rows[0]
            for j in range(1, PIVOTS):
                row = row - block[m][j] * rows[j]
            for j in some:
                row = jnp.where(at[j], block[m][j], row)
            new_rows.append(row)
            new = new - cols[m] * row
        ref[...] = new
        for m in some:
            ref[pl.ds(k + m, 1), :] = new_rows[m]
        return carry

    lax.fori_loop(0, 128 // PIVOTS, step, 0)


def dot(a, b):
    return jnp.dot(a, b, precision=HIGHEST, preferred_element_type=jnp.float32)


def dot(a, b):
    return jnp.dot(a, b, precision=HIGHEST, preferred_element_type=jnp.float32)


def column_slope(q, yp1, ym1, yp2, ym2, u12, v12):
    x = lax.broadcasted_iota(jnp.int32, (NX, NX), 0)
    xp1 = jnp.where(x < NX - 1, pltpu.roll(q, NX - 1, 0), 0.0)
    xm1 = jnp.where(x > 0, pltpu.roll(q, 1, 0), 0.0)
    xp2 = jnp.where(x < NX - 2, pltpu.roll(q, NX - 2, 0), 0.0)
    xm2 = jnp.where(x > 1, pltpu.roll(q, 2, 0), 0.0)
    along_x = 8.0 * (xp1 - xm1) - (xp2 - xm2)
    along_y = 8.0 * (yp1 - ym1) - (yp2 - ym2)
    laplace = xp1 + xm1 + yp1 + ym1 - 4.0 * q
    return 0.1 * laplace - u12 * along_x - v12 * along_y


def kernel(
    obs_in, c_in, u_in, v_in, var_in, out_ref,
    obs_row_ref, c_ref, u_ref, v_ref, var_ref, coef, q1, adv, aot, pieces, near, mid8, yt, rt, spart, sparts, srow, s_all, yg, yr, first, second,
    ext, mid, fore, theirs, ub, vb, qh, ql, zh, zl, chosen, send_sem, recv_sem, load_sem,
):
    f32, bf16 = jnp.float32, jnp.bfloat16
    g = lax.axis_index("grp")
    r = lax.axis_index("row")
    y, lo = g // 2, g % 2
    chip, core = r // 2, r % 2
    me = lo * MEMBERS + r

    loads = [
        pltpu.make_async_copy(source, target, load_sem.at[k])
        for k, (source, target) in enumerate(
            ((u_in, u_ref), (v_in, v_ref), (obs_in, obs_row_ref), (c_in, c_ref), (var_in, var_ref))
        )
    ]
    for load in loads:
        load.start()

    barrier = pltpu.get_barrier_semaphore()

    def greet(grp, row):
        pl.semaphore_signal(
            barrier, inc=1, device_id={"grp": grp, "row": row}, device_id_type=MESH
        )

    def greet_plane(i, carry):
        to = lax.rem(me + i, 2 * MEMBERS)
        greet(2 * y + to // MEMBERS, to % MEMBERS)
        return carry

    lax.fori_loop(1, 2 * MEMBERS, greet_plane, 0)
    across = jnp.where(lo == 0, g - 1, g + 1)
    has_across = (across >= 0) & (across < GROUPS)

    @pl.when(has_across)
    def _():
        def greet_across(i, carry):
            greet(across, i)
            return carry

        lax.fori_loop(0, MEMBERS, greet_across, 0)

    def greet_planes(i, carry):
        greet(lax.rem(2 * y + 2 + i // 2, GROUPS), 2 * chip + i % 2)
        return carry

    lax.fori_loop(0, 2 * GROUPS - 4, greet_planes, 0)
    on_diagonal = chip == g

    @pl.when(jnp.logical_not(on_diagonal))
    def _():
        greet(chip, 2 * g + core)

    for load in loads:
        load.wait()

    gx = lax.broadcasted_iota(jnp.int32, (NY, NX), 1)
    gy = lax.broadcasted_iota(jnp.int32, (NY, NX), 0)
    u12 = u_ref[...] * (1.0 / 12.0)
    v12 = v_ref[...] * (1.0 / 12.0)
    factors = (
        jnp.where(gx < NX - 1, 0.1 - 8.0 * u12, 0.0),
        jnp.where(gx > 0, 0.1 + 8.0 * u12, 0.0),
        jnp.where(gx < NX - 2, u12, 0.0),
        jnp.where(gx > 1, -u12, 0.0),
        jnp.where(gy < NY - 1, 0.1 - 8.0 * v12, 0.0),
        jnp.where(gy > 0, 0.1 + 8.0 * v12, 0.0),
        jnp.where(gy < NY - 2, v12, 0.0),
        jnp.where(gy > 1, -v12, 0.0),
    )
    for k in range(8):
        coef[k, 0:8] = jnp.zeros((8, NX), f32)
        coef[k, 128:136] = jnp.zeros((8, NX), f32)
        coef[k, 4 : 4 + NY] = factors[k]

    def factors_at(row):
        return [coef[k, pl.ds(row, 1), :] for k in range(8)]

    def read(ref, yy):
        return ref[:, lanes(jnp.clip(yy, 0, NY - 1))]

    def row_slope(ref, yy):
        return lane_slope(
            factors_at(yy + 4), read(ref, yy), read(ref, yy + 1), read(ref, yy - 1),
            read(ref, yy + 2), read(ref, yy - 2),
        )

    def row_first(yy, carry):
        q1[:, lanes(yy)] = c_ref[:, lanes(yy)] + row_slope(c_ref, yy)
        return carry

    cells = obs_row_ref[...]
    chosen_x = jnp.where(
        lax.broadcasted_iota(jnp.int32, (2 * NX, OBS), 0) % NX == cells % NX, 1.0, 0.0
    ).astype(bf16)
    cells_y = cells // NX

    def row_second(yy, acc):
        new = 0.5 * (c_ref[:, lanes(yy)] + q1[:, lanes(yy)] + row_slope(q1, yy))
        adv[:, lanes(yy)] = new
        high = new.astype(bf16)
        low = (new - high.astype(f32)).astype(bf16)
        found = jnp.dot(
            jnp.concatenate([high, low], axis=1), chosen_x, preferred_element_type=f32
        )
        return jnp.where(cells_y == yy, found, acc)

    lax.fori_loop(0, NY, row_first, 0, unroll=4)
    acc = lax.fori_loop(0, NY, row_second, jnp.zeros((ROWS, OBS), f32), unroll=4)

    quarter = r % 4
    place = lax.broadcasted_iota(jnp.int32, (NX, NX), 0) // ROWS == quarter
    for update in range(2):
        part = acc[:, update * NX : (update + 1) * NX]
        full = jnp.where(place, jnp.concatenate([part] * 4, axis=0), 0.0)
        aot[update * NX : (update + 1) * NX, :] = full.T

    pl.semaphore_wait(
        barrier,
        2 * MEMBERS - 1 + 2 * GROUPS - 4
        + jnp.where(has_across, MEMBERS, 0) + jnp.where(on_diagonal, 0, 1),
    )

    def some(to):
        return aot.at[pl.ds(pl.multiple_of(to * 8, 8), 8)]

    def share(i, carry):
        to = lax.rem(r + i, MEMBERS)
        remote(some(to), pieces.at[16 + r], send_sem.at[0], recv_sem.at[0], g, to).start()
        return carry

    lax.fori_loop(1, MEMBERS, share, 0)
    pltpu.make_async_copy(some(r), pieces.at[16 + r], recv_sem.at[0]).start()
    y_in = r // 4
    low = y_in < 4
    side = jnp.where(low, g - 1, g + 1)
    slot = jnp.where(low, 12 + y_in, y_in - 4) * 4 + quarter
    has_side = (side >= 0) & (side < GROUPS)

    @pl.when(has_side)
    def _():
        def share_side(i, carry):
            to = lax.rem(r + i, MEMBERS)
            remote(
                some(to), pieces.at[slot], send_sem.at[1], recv_sem.at[jnp.where(low, 2, 1)], side, to
            ).start()
            return carry

        lax.fori_loop(0, MEMBERS, share_side, 0)

    def my_columns(c):
        return adv.at[:, pl.ds(pl.multiple_of(r * 512 + lo * 256 + c * 128, 128), 128)]

    def arrival(c, source):
        outer = jnp.where(source < 16, source, source - 32)
        return jnp.where((source >= 16) & (source < 48), 7 + c, 17 + 32 * c + outer)

    def scatter(c, start, stop):
        def send(i, carry):
            to = lax.rem(me + STRIDE * i, 2 * MEMBERS)
            to_lo, to_r = to // MEMBERS, to % MEMBERS
            column = pl.multiple_of(to_r * 512 + to_lo * 256 + c * 128, 128)
            remote(
                adv.at[:, pl.ds(column, 128)], ext.at[c, 16 + me],
                send_sem.at[6 + c], recv_sem.at[arrival(c, me)], 2 * y + to_lo, to_r,
            ).start()
            return carry

        lax.fori_loop(start, stop, send, 0)

    for c in range(2):
        pltpu.make_async_copy(my_columns(c), ext.at[c, 16 + me], recv_sem.at[arrival(c, me)]).start()
    scatter(0, 1, FIRST_BATCH)

    ut = pltpu.roll(u12.T, lax.rem(2 * NX - 16 * y + 2, NX), 1)
    vt = pltpu.roll(v12.T, lax.rem(2 * NX - 16 * y + 2, NX), 1)
    for k in range(20):
        ub[k] = jnp.broadcast_to(ut[:, k : k + 1], (NX, NX))
        vb[k] = jnp.broadcast_to(vt[:, k : k + 1], (NX, NX))

    @pl.when(g == 0)
    def _():
        pieces[0:16] = jnp.zeros((16, 8, NX), f32)

    @pl.when(g == GROUPS - 1)
    def _():
        pieces[48:64] = jnp.zeros((16, 8, NX), f32)

    @pl.when(y == 0)
    def _():
        for c in range(2):
            ext[c, 0:16] = jnp.zeros((16, ROWS, NX), f32)

    @pl.when(y == 7)
    def _():
        for c in range(2):
            ext[c, 80:96] = jnp.zeros((16, ROWS, NX), f32)

    cell_at = lax.broadcasted_iota(jnp.int32, (1024, OBS), 0)
    chosen[...] = jnp.where(cell_at == obs_row_ref[...] - 1024 * g, 1.0, 0.0).astype(bf16)

    drain(pieces.at[16:48], recv_sem.at[0])

    @pl.when(g > 0)
    def _():
        drain(pieces.at[0:16], recv_sem.at[1])

    @pl.when(g < GROUPS - 1)
    def _():
        drain(pieces.at[48:64], recv_sem.at[2])

    for k in range(16):
        near[:, k * NX : (k + 1) * NX] = (
            pieces[4 * k] + pieces[4 * k + 1] + pieces[4 * k + 2] + pieces[4 * k + 3]
        )

    def at(ref, k):
        return ref[:, k * NX : (k + 1) * NX]

    def near_slope(ref, k):
        return lane_slope(
            factors_at(8 * g + k), at(ref, k), at(ref, k + 1), at(ref, k - 1),
            at(ref, k + 2), at(ref, k - 2),
        )

    for k in range(2, 14):
        mid8[:, k * NX : (k + 1) * NX] = at(near, k) + near_slope(near, k)
    for k in range(4, 12):
        yt[:, (k - 4) * NX : (k - 3) * NX] = 0.5 * (at(near, k) + at(mid8, k) + near_slope(mid8, k))

    whole = yt[...]
    high = whole.astype(bf16).astype(f32)
    middle = (whole - high).astype(bf16).astype(f32)
    stacked = jnp.concatenate(
        [high, middle, whole - high - middle, jnp.zeros((8, 1024), f32)], axis=0
    ).astype(bf16)
    parts = jnp.dot(stacked, chosen[...], preferred_element_type=f32)
    spart[...] = parts[0:8] + (parts[8:16] + parts[16:24])
    sparts[g] = spart[...]

    def to_groups(i, carry):
        to = lax.rem(g + i, GROUPS)
        remote(spart, sparts.at[g], send_sem.at[2], recv_sem.at[3], to, r).start()
        return carry

    lax.fori_loop(1, GROUPS, to_groups, 0)

    @pl.when(on_diagonal)
    def _():
        pltpu.make_async_copy(yt, rt, recv_sem.at[5]).start()

    @pl.when(jnp.logical_not(on_diagonal))
    def _():
        remote(yt, rt, send_sem.at[4], recv_sem.at[5], chip, 2 * g + core).start()

    yg[chip, core] = yt[...]
    scatter(0, FIRST_BATCH, SECOND_BATCH)
    scatter(1, 1, EARLY)
    drain(sparts.at[0:15], recv_sem.at[3])
    srow[...] = jnp.sum(sparts[...], axis=0)
    s_all[r] = srow[...]

    def block_row(i, carry):
        to = lax.rem(r + i, MEMBERS)
        remote(srow, s_all.at[r], send_sem.at[3], recv_sem.at[4], g, to).start()
        return carry

    lax.fori_loop(1, MEMBERS, block_row, 0)

    drain(rt, recv_sem.at[5])

    def to_columns(i, carry):
        grp = lax.rem(g + i // 2, GROUPS)
        half = lax.rem(core + i, 2)
        remote(
            rt.at[:, pl.ds(pl.multiple_of(half * 512, 512), 512)], yr.at[2 * g + core],
            send_sem.at[8], recv_sem.at[9], grp, 2 * chip + half,
        ).start()
        return carry

    lax.fori_loop(1, 2 * GROUPS, to_columns, 0)
    pltpu.make_async_copy(
        rt.at[:, pl.ds(pl.multiple_of(core * 512, 512), 512)], yr.at[2 * g + core], recv_sem.at[9]
    ).start()

    scatter(0, SECOND_BATCH, 2 * MEMBERS)
    scatter(1, EARLY, 2 * MEMBERS)

    def to_group(i, carry):
        to = lax.rem(r + 2 * i, MEMBERS)
        remote(yt, yg.at[chip, core], send_sem.at[5], recv_sem.at[6], g, to).start()
        return carry

    lax.fori_loop(1, GROUPS, to_group, 0)

    drain(s_all.at[0:31], recv_sem.at[4])
    diagonal = lax.broadcasted_iota(jnp.int32, (128, 128), 0) == lax.broadcasted_iota(
        jnp.int32, (128, 128), 1
    )
    s11 = s_all[0:16, :, 0:128].reshape(128, 128)
    first[...] = 0.5 * (s11 + s11.T) + jnp.where(diagonal, var_ref[0:1, :], 0.0)
    negative_inverse(first)

    relay = remote(
        yg.at[:, core], yg.at[:, core], send_sem.at[9], recv_sem.at[10], g, 2 * chip + 1 - core
    )

    def trade(c):
        return remote(
            fore.at[c, 1 - lo], theirs.at[c], send_sem.at[14 + c], recv_sem.at[15 + c],
            2 * y + 1 - lo, r,
        )

    def forward(c, start, stop):
        def step(i, carry):
            source = lax.rem(me + (2 * MEMBERS - STRIDE) * i, 2 * MEMBERS)
            block = ext.at[c, 16 + source]

            @pl.when((source < 16) | (source >= 48))
            def _():
                drain(block, recv_sem.at[arrival(c, source)])

            @pl.when((source < 16) & (y > 0))
            def _():
                remote(
                    block, ext.at[c, 80 + source], send_sem.at[12 + c], recv_sem.at[13 + c], g - 2, r
                ).start()

            @pl.when((source >= 48) & (y < 7))
            def _():
                remote(
                    block, ext.at[c, source - 48], send_sem.at[10 + c], recv_sem.at[11 + c], g + 2, r
                ).start()

            return carry

        lax.fori_loop(start, stop, step, 0)

    forward(0, 0, 2 * MEMBERS)

    s12 = s_all[0:16, :, 128:256].reshape(128, 128)
    s21 = s_all[16:32, :, 0:128].reshape(128, 128)
    s22 = s_all[16:32, :, 128:256].reshape(128, 128)
    inner = s22 + dot(s21, dot(first[...], s12))
    second[...] = 0.5 * (inner + inner.T) + jnp.where(diagonal, var_ref[1:2, :], 0.0)
    negative_inverse(second)
    def grid_row(c, k):
        return jnp.concatenate([ext[c, 4 * k + i] for i in range(4)], axis=0)

    def column_first(c, start, stop):
        def step(k, carry):
            q = grid_row(c, k)
            inside = (y * 16 + k - 4 >= 0) & (y * 16 + k - 4 < NY)
            slope = column_slope(
                q, grid_row(c, k + 1), grid_row(c, k - 1), grid_row(c, k + 2), grid_row(c, k - 2),
                ub[k - 2], vb[k - 2],
            )
            mid[k - 2] = jnp.where(inside, q + slope, 0.0)
            return carry

        lax.fori_loop(start, stop, step, 0)

    def column_second(c, half):
        def step(j, carry):
            k = half * 8 + j + 4
            q = mid[k - 2]
            slope = column_slope(
                q, mid[k - 1], mid[k - 3], mid[k], mid[k - 4], ub[k - 2], vb[k - 2]
            )
            fore[c, half, j] = 0.5 * (grid_row(c, k) + q + slope)
            return carry

        lax.fori_loop(0, 8, step, 0)

    def correct(column, field):
        cols = pl.ds(pl.multiple_of(column, 256), 256)
        b_high, b_low = zh[:, cols], zl[:, cols]

        def part(a, b):
            return jnp.dot(a, b, preferred_element_type=f32)

        def step(i, carry):
            rows = pl.ds(pl.multiple_of(i * 256, 256), 256)
            a_high, a_low = qh[rows, :], ql[rows, :]
            product = part(a_high, b_high) + (part(a_high, b_low) + part(a_low, b_high))
            for c in range(2):
                for k in range(2):
                    j = 2 * i + k
                    place = pl.ds(pl.multiple_of(column + c * 128, 128), 128)
                    out_ref[pl.ds(pl.multiple_of(j * NX, NX), NX), place] = (
                        field(c, j) - product[k * 128 : (k + 1) * 128, c * 128 : (c + 1) * 128]
                    )
            return carry

        lax.fori_loop(0, 4, step, 0)

    forward(1, 0, 32)
    for c in range(2):
        if c == 1:
            forward(1, 32, 2 * MEMBERS)
        drain(ext.at[c, 32:64], recv_sem.at[7 + c])
        column_first(c, 6, 18)
        @pl.when(y > 0)
        def _():
            drain(ext.at[c, 0:16], recv_sem.at[11 + c])

        @pl.when(y < 7)
        def _():
            drain(ext.at[c, 80:96], recv_sem.at[13 + c])

        column_first(c, 2, 6)
        column_first(c, 18, 22)
        column_second(c, 1 - lo)
        trade(c).start()
        column_second(c, lo)

    drain(yg.at[0:15, 0], recv_sem.at[6])
    relay.start()
    drain(yr, recv_sem.at[9])
    r1 = yr[0:16].reshape(128, 512)
    r2 = yr[16:32].reshape(128, 512)
    z2 = -dot(second[...], r2 + dot(s21, dot(first[...], r1)))
    z1 = -dot(first[...], r1 - dot(s12, z2))
    for k, z in ((0, z1), (1, z2)):
        high = z.astype(bf16)
        zh[k * 128 : (k + 1) * 128, :] = high
        zl[k * 128 : (k + 1) * 128, :] = (z - high.astype(f32)).astype(bf16)
    relay.wait_recv()
    for j in range(8):
        q = yg[:, :, :, j * NX : (j + 1) * NX].reshape(OBS, NX).T
        high = q.astype(bf16)
        qh[j * NX : (j + 1) * NX] = high
        ql[j * NX : (j + 1) * NX] = (q - high.astype(f32)).astype(bf16)
    correct(lo * 256, lambda c, j: fore[c, lo, j])
    correct((1 - lo) * 256, lambda c, j: 0.0)
    for c in range(2):
        trade(c).wait_recv()

        def finish(j, carry):
            rows = pl.ds(pl.multiple_of(j * NX, NX), NX)
            place = pl.ds(pl.multiple_of((1 - lo) * 256 + c * 128, 128), 128)
            out_ref[rows, place] = out_ref[rows, place] + theirs[c, j]
            return carry

        lax.fori_loop(0, 8, finish, 0)

    drain(pieces.at[0:31], send_sem.at[0])

    @pl.when(has_side)
    def _():
        drain(pieces.at[0:32], send_sem.at[1])

    drain(sparts.at[0:15], send_sem.at[2])
    drain(s_all.at[0:31], send_sem.at[3])

    @pl.when(jnp.logical_not(on_diagonal))
    def _():
        drain(rt, send_sem.at[4])

    drain(yg.at[0:15, 0], send_sem.at[5])
    drain(yr.at[0:31], send_sem.at[8])
    relay.wait_send()
    for c in range(2):
        drain(ext.at[c, 0:63], send_sem.at[6 + c])
        trade(c).wait_send()

        @pl.when(y < 7)
        def _():
            drain(ext.at[c, 0:16], send_sem.at[10 + c])

        @pl.when(y > 0)
        def _():
            drain(ext.at[c, 80:96], send_sem.at[12 + c])


def local(cov_prior, courant_x_field, courant_y_field, obs_cells, obs_var):
    f32, bf16 = jnp.float32, jnp.bfloat16
    scratch = [
        ((1, OBS), jnp.int32),
        ((ROWS, NCELL), f32),
        ((NY, NX), f32),
        ((NY, NX), f32),
        ((2, NX), f32),
        ((8, 136, NX), f32),
        ((ROWS, NCELL), f32),
        ((ROWS, NCELL), f32),
        ((OBS, NX), f32),
        ((64, 8, NX), f32),
        ((8, 2048), f32),
        ((8, 2048), f32),
        ((8, 1024), f32),
        ((8, 1024), f32),
        ((8, OBS), f32),
        ((GROUPS, 8, OBS), f32),
        ((8, OBS), f32),
        ((MEMBERS, 8, OBS), f32),
        ((GROUPS, 2, 8, 1024), f32),
        ((MEMBERS, 8, 512), f32),
        ((128, 128), f32),
        ((128, 128), f32),
        ((2, 96, ROWS, NX), f32),
        ((20, NX, NX), f32),
        ((2, 2, 8, NX, NX), f32),
        ((2, 8, NX, NX), f32),
        ((20, NX, NX), f32),
        ((20, NX, NX), f32),
        ((1024, OBS), bf16),
        ((1024, OBS), bf16),
        ((OBS, 512), bf16),
        ((OBS, 512), bf16),
        ((1024, OBS), bf16),
    ]
    return pl.pallas_call(
        kernel,
        out_shape=jax.ShapeDtypeStruct((1024, 512), f32),
        in_specs=[pl.BlockSpec(memory_space=pltpu.HBM)] * 5,
        out_specs=VMEM,
        scratch_shapes=[pltpu.VMEM(shape, dtype) for shape, dtype in scratch]
        + [pltpu.SemaphoreType.DMA((16,)), pltpu.SemaphoreType.DMA((81,)), pltpu.SemaphoreType.DMA((5,))],
        compiler_params=pltpu.CompilerParams(
            collective_id=0, has_side_effects=True, vmem_limit_bytes=VMEM_LIMIT
        ),
    )(obs_cells.reshape(1, OBS), cov_prior, courant_x_field, courant_y_field, obs_var)


def solution(mesh):
    placed = (P(("grp", "row"), None), P(), P(), P(), P())
    return jax.shard_map(
        local, mesh=mesh, in_specs=placed, out_specs=P("grp", "row"), check_vma=False
    )
```
